32 devices in a mesh: row: 4 (over y, x), col: 8 (over z, core).
Axes of the slice: x: 2, y: 2, z: 4, core: 2. Of those that a mesh axis runs over, the one named last changes fastest.
Arguments:
- features: bfloat16 [16384, 256], P(('row', 'col')), may hold values from -6 to 6
- weight: bfloat16 [256, 256], replicated, may hold values from -0.375 to 0.375
- adjacency: bfloat16 [4, 8, 384, 128, 128], P('row', 'col'), may hold values from -0.0546875 to 0.0546875
- block_rows: int32 [4, 8, 384], P('row', 'col'), may hold values from 0 to 31
- block_cols: int32 [4, 8, 384], P('row', 'col'), may hold values from 0 to 15
- live_blocks: int32 [4, 8], P('row', 'col'), may hold values from 96 to 384, as said below
- part_gains: float32 [16, 256], replicated, may hold values from 0.5 to 2
- partition: int32 [16384], P(('row', 'col')), may hold values from 0 to 15, never falling along the last dimension, each value on 1 to 2048 neighbouring positions
- cotangent: bfloat16 [16384, 256], P(('row', 'col')), may hold values from -6 to 6
Outputs:
- layer_out: bfloat16 [16384, 256], P(('row', 'col'))
- feature_grad: bfloat16 [16384, 256], P(('row', 'col'))
- weight_grad: float32 [256, 256], replicated
- gain_grad: float32 [16, 256], replicated
The draws below stay inside these ranges and needn't reach their ends.
Inputs may be any that keep to these rules, and one draw needn't show every extreme that they name: Only the first live_blocks[i, j] slots of tile (i, j) are used; some tile uses all 384 slots. partition numbers never fall along the nodes; every partition has 1 to 2048 nodes, one exactly that many.
All inputs are finite; a program needn't handle non-finite values.
Results may differ from the reference program's by a relative error of at most 0.024.
Values may be sent and summed in bfloat16 or wider, within the bound.
No kernel may reach another device: no remote copies, remote signals or barrier semaphores. Data moves between devices by JAX's collectives and lax.ppermute only.
A program may use at most 128 MiB of HBM per device.

```python
import math
import jax
import jax.numpy as jnp
import numpy as np
from jax import lax

WIDTH = 256
BLOCK = 128
NODE_DEV = 512
SLOTS = 384
GRID_ROWS = 4
GRID_COLS = 8
NODES = 16384
ROW_BLOCKS = 32
COL_BLOCKS = 16
PARTS_SIZE = 16


def draw_live_blocks(key, part):
    first_key, second_key = jax.random.split(jax.random.fold_in(key, 7))
    tile_total = GRID_ROWS * GRID_COLS
    drawn = jax.random.randint(first_key, (tile_total,), SLOTS // 4, SLOTS + 1)
    chosen = jax.random.randint(second_key, (), 0, tile_total)
    filled = jnp.where(jnp.arange(tile_total) == chosen, SLOTS, drawn)
    return filled.reshape(GRID_ROWS, GRID_COLS).astype(jnp.int32)


def set_ends(array, key, least, high):
    index_at = [jax.random.randint(jax.random.fold_in(key, axis), (), 0, length) for axis, length in enumerate(array.shape)]
    main_axis = array.shape.index(max(array.shape))
    next_to = index_at[:main_axis] + [(index_at[main_axis] + 1) % array.shape[main_axis]] + index_at[main_axis + 1:]
    return array.at[tuple(index_at)].set(least).at[tuple(next_to)].set(high)


def levels(stream_key, dims, pieces, low, high):
    factor_of, own = 1.0, jax.random.fold_in(stream_key, 6)
    for axis_at, parts in pieces:
        steps = jnp.exp(jax.random.uniform(jax.random.fold_in(own, axis_at), (parts,), jnp.float32, low / len(pieces), high / len(pieces)))
        factor_of = factor_of * jnp.repeat(steps, dims[axis_at] // parts).reshape([-1 if axis == axis_at else 1 for axis in range(len(dims))])
    return factor_of


def rank_bounds(number_of, skew):
    portions = [(1 << 20) // math.isqrt(grade ** skew) + 1 for grade in range(1, number_of + 1)]
    scale = 1 + sum(portions) // (1 << 30)
    return np.cumsum(np.array([max(1, weight // scale) for weight in portions]))


def ranked(key, extent, amount, lean):
    grid = rank_bounds(amount, lean)
    ticket = jax.random.randint(jax.random.fold_in(key, 1), extent, 0, int(grid[amount - 1]))
    standing = jnp.searchsorted(jnp.asarray(grid, jnp.int32), ticket, side="right")
    return jax.random.permutation(jax.random.fold_in(key, 2), amount)[standing].astype(jnp.int32)


def profile(count, total, bound, lean):
    portions = [(1 << 20) // math.isqrt(rank ** lean) + 1 for rank in range(2, count + 1)]
    spare, counts = total - bound - (count - 1), [1] * (count - 1)
    while spare > 0:
        movable = [i for i in range(count - 1) if counts[i] < bound]
        whole, remaining = sum([portions[i] for i in movable]), spare
        for i in movable:
            extra = min(bound - counts[i], max(1, remaining * portions[i] // whole), spare)
            counts[i] = counts[i] + extra
            spare = spare - extra
    return np.array([bound] + counts)


def ragged_sizes(own_key, count, total, reach, lean):
    if count == 2:
        one = jax.random.randint(own_key, (), max(1, total - reach), min(reach, total - 1) + 1)
        return jnp.stack([one, total - one])
    sizes = jnp.asarray(profile(count, total, reach, lean), jnp.int32)
    twos = (count - 1) // 2
    source_of, sink = sizes[1:1 + 2 * twos:2], sizes[2:2 + 2 * twos:2]
    slack = jnp.minimum(source_of - 1, reach - sink)
    shifted = jax.random.randint(jax.random.fold_in(own_key, 1), (twos,), 0, 1 << 20) % (slack + 1)
    sizes = sizes.at[1:1 + 2 * twos:2].set(source_of - shifted).at[2:2 + 2 * twos:2].set(sink + shifted)
    return sizes[jax.random.permutation(jax.random.fold_in(own_key, 2), count)]


def normal_values(stream_key, shape, deviation, limit, cuts=(), kind=jnp.bfloat16):
    result = deviation * jax.random.normal(stream_key, shape, jnp.float32)
    if cuts:
        result = result * levels(stream_key, shape, cuts, -0.22, 0.18)
    return jnp.clip(result, -limit, limit).astype(kind)


def setup_inputs(seed: int = 0) -> dict:
    arg_keys = jax.random.split(jax.random.key(seed), 10)
    features = normal_values(arg_keys[0], (NODES, WIDTH), 1.0, 6.0, ((0, 32),))
    weight = normal_values(arg_keys[1], (WIDTH, WIDTH), WIDTH ** -0.5, 0.375)
    adjacency = normal_values(arg_keys[2], (GRID_ROWS, GRID_COLS, SLOTS, BLOCK, BLOCK), (BLOCK * BLOCK * SLOTS // NODE_DEV) ** -0.5, 0.0546875, ((0, 4), (1, 8)))
    block_rows = set_ends(ranked(arg_keys[3], (GRID_ROWS, GRID_COLS, SLOTS), ROW_BLOCKS, 1), jax.random.fold_in(arg_keys[3], 3), 0, ROW_BLOCKS - 1).astype(jnp.int32)
    block_cols = set_ends(jax.random.randint(arg_keys[4], (GRID_ROWS, GRID_COLS, SLOTS), 0, COL_BLOCKS), jax.random.fold_in(arg_keys[4], 1), 0, COL_BLOCKS - 1).astype(jnp.int32)
    live_blocks = draw_live_blocks(jax.random.fold_in(arg_keys[9], 71), 0)
    part_gains = jnp.clip(jnp.exp(jax.random.uniform(arg_keys[6], (PARTS_SIZE, WIDTH), jnp.float32, math.log(0.5), math.log(2.0))), 0.5, 2.0)
    partition = jnp.searchsorted(jnp.cumsum(ragged_sizes(arg_keys[7], PARTS_SIZE, NODES, 4 * NODE_DEV, 1)), jnp.arange(NODES), side="right").astype(jnp.int32)
    cotangent = normal_values(arg_keys[8], (NODES, WIDTH), 1.0, 6.0, ((0, 32),))
    return {"features": features, "weight": weight, "adjacency": adjacency, "block_rows": block_rows, "block_cols": block_cols, "live_blocks": live_blocks, "part_gains": part_gains, "partition": partition, "cotangent": cotangent}


def silu_slope(values):
    sig = jax.nn.sigmoid(values)
    return sig * (1.0 + values * (1.0 - sig))

def rounded(values):
    return lax.optimization_barrier(values.astype(jnp.bfloat16)).astype(jnp.float32)

def tile_sum(tile_values, row_index, col_index, live_count, panels, out_blocks, forward):
    slot_mask = (jnp.arange(SLOTS, dtype=jnp.int32) < live_count).astype(jnp.float32)
    weights = tile_values.astype(jnp.float32) * slot_mask[:, None, None]
    panel_blocks = panels.astype(jnp.float32).reshape(-1, BLOCK, WIDTH)
    if forward:
        products = jnp.einsum('kab,kbf->kaf', weights, panel_blocks[col_index])
        targets = row_index
    else:
        products = jnp.einsum('kab,kaf->kbf', weights, panel_blocks[row_index])
        targets = col_index
    totals = jnp.zeros((out_blocks, BLOCK, WIDTH), jnp.float32).at[targets].add(products)
    return totals.reshape(out_blocks * BLOCK, WIDTH)

def reference(features, weight, adjacency, block_rows, block_cols, live_blocks, part_gains, partition, cotangent):
    hidden = jnp.dot(features, weight, preferred_element_type=jnp.float32).astype(jnp.bfloat16)
    hidden_grid = hidden.reshape(GRID_ROWS, GRID_COLS, NODE_DEV, WIDTH)

    def forward_tile(position, running):
        tile_row = position // GRID_COLS
        tile_col = position % GRID_COLS
        panels = hidden_grid[:, tile_col].reshape(GRID_ROWS * NODE_DEV, WIDTH)
        part_sum = tile_sum(adjacency[tile_row, tile_col], block_rows[tile_row, tile_col], block_cols[tile_row, tile_col], live_blocks[tile_row, tile_col], panels, ROW_BLOCKS, True)
        return running.at[tile_row].add(rounded(part_sum))
    row_sums = lax.fori_loop(0, GRID_ROWS * GRID_COLS, forward_tile, jnp.zeros((GRID_ROWS, GRID_COLS * NODE_DEV, WIDTH), jnp.float32))
    summed = row_sums.reshape(NODES, WIDTH)
    activated = jax.nn.silu(summed)
    row_gains = part_gains[partition]
    layer_out = (activated * row_gains).astype(jnp.bfloat16)
    agg_grad = (cotangent.astype(jnp.float32) * row_gains * silu_slope(summed)).astype(jnp.bfloat16)
    grad_grid = agg_grad.reshape(GRID_ROWS, GRID_COLS * NODE_DEV, WIDTH)

    def backward_tile(position, running):
        tile_row = position // GRID_COLS
        tile_col = position % GRID_COLS
        part_sum = tile_sum(adjacency[tile_row, tile_col], block_rows[tile_row, tile_col], block_cols[tile_row, tile_col], live_blocks[tile_row, tile_col], grad_grid[tile_row], COL_BLOCKS, False)
        return running.at[tile_col].add(rounded(part_sum))
    col_sums = lax.fori_loop(0, GRID_ROWS * GRID_COLS, backward_tile, jnp.zeros((GRID_COLS, GRID_ROWS * NODE_DEV, WIDTH), jnp.float32))
    hidden_grad = col_sums.reshape(GRID_COLS, GRID_ROWS, NODE_DEV, WIDTH).transpose(1, 0, 2, 3).reshape(NODES, WIDTH).astype(jnp.bfloat16)
    feature_grad = jnp.dot(hidden_grad, weight.T, preferred_element_type=jnp.float32).astype(jnp.bfloat16)
    weight_grad = jnp.dot(features.T, hidden_grad, preferred_element_type=jnp.float32) / jnp.sqrt(jnp.float32(NODES))
    part_sums = jax.ops.segment_sum(cotangent.astype(jnp.float32) * activated, partition, num_segments=PARTS_SIZE)
    sizes_part = jax.ops.segment_sum(jnp.ones((NODES,), jnp.float32), partition, num_segments=PARTS_SIZE)
    gain_grad = part_sums / jnp.sqrt(sizes_part)[:, None]
    return (layer_out, feature_grad, weight_grad, gain_grad)
```

```python
import functools

import jax
import jax.numpy as jnp
from jax import lax
from jax.experimental import pallas as pl
from jax.experimental.pallas import tpu as pltpu
from jax.sharding import PartitionSpec as P

BLOCK = 128
GROUP = 16
BUFFERS = 8
HEAVY = 16
MIB = 1 << 20


def bits_of(count):
    return [1 << b for b in range(count.bit_length() - 1)]


def halving_order(count):
    if count == 1:
        return [0]
    evens = [2 * k for k in halving_order(count // 2)]
    return [k ^ 1 for k in evens] + evens


def build_kernel(
    live_ref, rows_ref, cols_ref, place_row_ref, place_col_ref, slots_ref, tile_ref, buf, total, counts, sems
):
    live = live_ref[0]
    groups = (live + GROUP - 1) // GROUP
    col_blocks = tile_ref.shape[1] // BLOCK

    def fetch(group, slot):
        return pltpu.make_async_copy(
            slots_ref.at[pl.ds(group * GROUP, GROUP)], buf.at[slot], sems.at[slot]
        )

    for b in range(BUFFERS):
        @pl.when(b < groups)
        def _():
            fetch(b, b).start()

    zeros = jnp.zeros((BLOCK, tile_ref.shape[1]), tile_ref.dtype)

    @pl.loop(0, tile_ref.shape[0] // BLOCK)
    def _(r):
        tile_ref[pl.ds(pl.multiple_of(r * BLOCK, BLOCK), BLOCK), :] = zeros

    def place(index):
        top = pl.multiple_of(rows_ref[index] * BLOCK, BLOCK)
        left = pl.multiple_of(cols_ref[index] * BLOCK, BLOCK)
        return pl.ds(top, BLOCK), pl.ds(left, BLOCK)

    @pl.loop(0, groups)
    def _(group):
        slot = lax.rem(group, BUFFERS)
        fetch(group, slot).wait()

        @pl.loop(0, jnp.minimum(GROUP, live - group * GROUP))
        def _(s):
            at = place(group * GROUP + s)
            tile_ref[at] += buf[slot, s]

        @pl.when(group + BUFFERS < groups)
        def _():
            fetch(group + BUFFERS, slot).start()

    slot_total = place_row_ref.shape[1]
    live_here = lax.broadcasted_iota(jnp.int32, (1, slot_total), 1) < live
    same = jnp.where(
        (place_row_ref[...] == place_col_ref[...]) & live_here, 1.0, 0.0
    )
    most = jnp.max(jnp.sum(same, axis=1, keepdims=True))

    @pl.when(most > HEAVY)
    def _():
        @pl.loop(0, counts.shape[0])
        def _(p):
            counts[p] = 0

        @pl.loop(0, live)
        def _(index):
            p = rows_ref[index] * col_blocks + cols_ref[index]
            counts[p] = counts[p] + 1

        @pl.loop(0, live)
        def _(index):
            p = rows_ref[index] * col_blocks + cols_ref[index]

            @pl.when(counts[p] > HEAVY)
            def _():
                counts[p] = 0
                total[...] = jnp.zeros_like(total)

                @pl.loop(index, live)
                def _(other):
                    @pl.when(rows_ref[other] * col_blocks + cols_ref[other] == p)
                    def _():
                        copy = pltpu.make_async_copy(
                            slots_ref.at[pl.ds(other, 1)], buf.at[0, pl.ds(0, 1)], sems.at[0]
                        )
                        copy.start()
                        copy.wait()
                        total[...] += buf[0, 0].astype(jnp.float32)

                tile_ref[place(index)] = total[...].astype(tile_ref.dtype)


def build_tile(slots, rows, cols, live, row_blocks, col_blocks):
    places = rows * col_blocks + cols
    smem = pl.BlockSpec(memory_space=pltpu.SMEM)
    vmem = pl.BlockSpec(memory_space=pltpu.VMEM)
    slot_total = slots.shape[0]
    return pl.pallas_call(
        build_kernel,
        out_shape=pltpu.VMEM((row_blocks * BLOCK, col_blocks * BLOCK), jnp.bfloat16),
        in_specs=[smem, smem, smem, vmem, vmem, pl.BlockSpec(memory_space=pl.ANY)],
        out_specs=vmem,
        scratch_shapes=[
            pltpu.VMEM((BUFFERS, GROUP, BLOCK, BLOCK), jnp.bfloat16),
            pltpu.VMEM((BLOCK, BLOCK), jnp.float32),
            pltpu.SMEM((row_blocks * col_blocks,), jnp.int32),
            pltpu.SemaphoreType.DMA((BUFFERS,)),
        ],
        compiler_params=pltpu.CompilerParams(vmem_limit_bytes=12 * MIB),
        cost_estimate=pl.CostEstimate(flops=0, bytes_accessed=20 * MIB, transcendentals=0),
        name="build_tile",
    )(live, rows, cols, places[None, :], places[:, None], slots)


def forward_kernel(order, *refs):
    at_ref, tile_ref, weight_ref = refs[:3]
    chunks = 2
    feature_refs = refs[3 : -1 - 2 * chunks]
    send_refs, rest_refs = refs[-1 - 2 * chunks : -1 - chunks], refs[-1 - chunks : -1]
    hidden = refs[-1]
    own_row, own_col = at_ref[0], at_ref[1]
    share = feature_refs[0].shape[0]
    for r, feature_ref in enumerate(feature_refs):
        at = pl.ds(pl.multiple_of((own_row ^ r) * share, share), share)
        hidden[at, :] = jnp.dot(
            feature_ref[...], weight_ref[...], preferred_element_type=jnp.float32
        ).astype(jnp.bfloat16)
    half = len(order) // 2
    width = hidden.shape[1] // chunks
    step = share // 2
    for t, k in enumerate(order):
        base = (own_col ^ k) * share
        into = send_refs if t < half else rest_refs
        for m in range(0, share, step):
            at = pl.ds(pl.multiple_of(base + m, step), step)
            product = jnp.dot(tile_ref[at, :], hidden[...], preferred_element_type=jnp.float32)
            product = product.astype(jnp.bfloat16)
            to = pl.ds((t % half) * share + m, step)
            for c in range(chunks):
                into[c][to, :] = product[:, c * width : (c + 1) * width]


def forward(at, tile, weight, features, order):
    share, width = features[0].shape
    half = len(order) // 2
    part = pltpu.VMEM((half * share, width // 2), jnp.bfloat16)
    vmem = pl.BlockSpec(memory_space=pltpu.VMEM)
    smem = pl.BlockSpec(memory_space=pltpu.SMEM)
    return pl.pallas_call(
        functools.partial(forward_kernel, order),
        out_shape=[part] * 4,
        in_specs=[smem] + [vmem] * (2 + len(features)),
        out_specs=[vmem] * 4,
        scratch_shapes=[pltpu.VMEM((len(features) * share, width), jnp.bfloat16)],
        compiler_params=pltpu.CompilerParams(vmem_limit_bytes=12 * MIB),
        cost_estimate=pl.CostEstimate(
            flops=2 * tile.shape[0] * tile.shape[1] * width, bytes_accessed=0, transcendentals=0
        ),
        name="forward",
    )(at, tile, weight, *features)


def backward_kernel(orders, row_count, *refs):
    at_ref, tile_ref = refs[:2]
    grad_refs = refs[2 : 2 + len(orders)]
    feature_refs = refs[2 + len(orders) : 2 + len(orders) + row_count]
    part_refs = refs[-2 - row_count : -2]
    weight_ref, turned = refs[-2:]
    own_row, own_col = at_ref[0], at_ref[1]
    share = feature_refs[0].shape[0]
    for order, grad_ref in zip(orders, grad_refs):
        for t, k in enumerate(order):
            at = pl.ds(pl.multiple_of((own_col ^ k) * share, share), share)
            turned[:, at] = grad_ref[t * share : (t + 1) * share, :].T
    total = None
    for r in range(row_count):
        at = pl.ds(pl.multiple_of((own_row ^ r) * share, share), share)
        product = jnp.dot(turned[...], tile_ref[:, at], preferred_element_type=jnp.float32)
        product = product.astype(jnp.bfloat16)
        part_refs[r][...] = product
        term = jnp.dot(product, feature_refs[r][...], preferred_element_type=jnp.float32)
        total = term if total is None else total + term
    weight_ref[...] = total


def backward(at, tile, grads, orders, features):
    share, width = features[0].shape
    chunk = grads[0].shape[1]
    rows = len(features)
    vmem = pl.BlockSpec(memory_space=pltpu.VMEM)
    smem = pl.BlockSpec(memory_space=pltpu.SMEM)
    return pl.pallas_call(
        functools.partial(backward_kernel, orders, rows),
        out_shape=[pltpu.VMEM((chunk, share), jnp.bfloat16)] * rows
        + [pltpu.VMEM((chunk, width), jnp.float32)],
        in_specs=[smem] + [vmem] * (1 + len(grads) + rows),
        out_specs=[vmem] * (rows + 1),
        scratch_shapes=[pltpu.VMEM((chunk, tile.shape[0]), jnp.bfloat16)],
        compiler_params=pltpu.CompilerParams(vmem_limit_bytes=12 * MIB),
        cost_estimate=pl.CostEstimate(
            flops=4 * tile.shape[0] * tile.shape[1] * chunk, bytes_accessed=0, transcendentals=0
        ),
        name="backward",
    )(at, tile, *grads, *features)


def silu_slope(values):
    sig = jax.nn.sigmoid(values)
    return sig * (1.0 + values * (1.0 - sig))


def swap(values, axis, mask, count):
    return lax.ppermute(values, axis, [(d, d ^ mask) for d in range(count)])


def dense_device(
    row_count,
    col_count,
    features,
    weight,
    adjacency,
    block_rows,
    block_cols,
    live_blocks,
    part_gains,
    partition,
    cotangent,
):
    share, width = features.shape
    chunk = width // 2
    at = jnp.stack([lax.axis_index("row"), lax.axis_index("col")]).astype(jnp.int32)
    gathered = [features] + [swap(features, "row", r, row_count) for r in range(1, row_count)]
    tile = build_tile(
        adjacency[0, 0],
        block_rows[0, 0],
        block_cols[0, 0],
        live_blocks[0],
        share * col_count // BLOCK,
        share * row_count // BLOCK,
    )
    member = (
        partition[:, None] == jnp.arange(part_gains.shape[0], dtype=jnp.int32)[None, :]
    ).astype(jnp.float32)
    row_gains = jnp.dot(member, part_gains, precision=lax.Precision.HIGHEST)
    upstream = cotangent.astype(jnp.float32) * row_gains

    order = halving_order(col_count)
    col_bits = bits_of(col_count)
    *parts, = forward(at, tile, weight, gathered, order)
    sends, rests = parts[:2], parts[2:]

    def wide(values):
        return values.astype(jnp.float32)

    summed, hidden_parts, weight_parts = [], [], []
    for c in range(2):
        arrived = [swap(sends[c], "col", col_bits[0], col_count)]
        rest = rests[c]
        for bit in col_bits[1:]:
            first = sum(wide(a[-rest.shape[0] :][: rest.shape[0] // 2]) for a in arrived)
            half = rest.shape[0] // 2
            out = (wide(rest[:half]) + first).astype(jnp.bfloat16)
            arrived.append(swap(out, "col", bit, col_count))
            rest = rest[half:]
        total = wide(rest)
        for a in arrived:
            total = total + wide(a[-share:])
        summed.append(total)
        grad = (upstream[:, c * chunk : (c + 1) * chunk] * silu_slope(total)).astype(jnp.bfloat16)
        held, orders = [grad], [[0]]
        for bit in reversed(col_bits[1:]):
            sent = held[0] if len(held) == 1 else jnp.concatenate(held[::-1], axis=0)
            held.append(swap(sent, "col", bit, col_count))
            orders.append([k ^ bit for o in orders[::-1] for k in o])
        bit = col_bits[0]
        for h, o in list(zip(held, orders)):
            held.append(swap(h, "col", bit, col_count))
            orders.append([k ^ bit for k in o])
        *hidden_part, weight_part = backward(at, tile, held, orders, gathered)
        for r in range(1, row_count):
            hidden_part[r] = swap(hidden_part[r], "row", r, row_count)
        hidden_parts.append(hidden_part)
        weight_parts.append(weight_part)

    summed = jnp.concatenate(summed, axis=1)
    activated = jax.nn.silu(summed)
    layer_out = (activated * row_gains).astype(jnp.bfloat16)

    hidden_grad = jnp.concatenate([sum(wide(p) for p in ps) for ps in hidden_parts], axis=0)
    feature_grad = lax.dot_general(
        hidden_grad.astype(jnp.bfloat16),
        weight,
        (((0,), (1,)), ((), ())),
        preferred_element_type=jnp.float32,
    ).astype(jnp.bfloat16)

    part_terms = jnp.dot(
        member.T, wide(cotangent) * activated, precision=lax.Precision.HIGHEST
    )
    part_sizes = jnp.broadcast_to(jnp.sum(member, axis=0)[:, None], (member.shape[1], width))
    totals = jnp.concatenate(weight_parts + [part_terms, part_sizes], axis=0)
    for bit in col_bits[1:] + col_bits[:1]:
        totals = totals + swap(totals, "col", bit, col_count)
    for bit in bits_of(row_count):
        totals = totals + swap(totals, "row", bit, row_count)
    total_nodes = share * row_count * col_count
    weight_grad = totals[:width].T / jnp.sqrt(jnp.float32(total_nodes))
    part_count = member.shape[1]
    gain_grad = totals[width : width + part_count] / jnp.sqrt(totals[width + part_count :])
    return (layer_out, feature_grad, weight_grad, gain_grad)


def slot_sum(tile_values, row_index, col_index, live_count, panels, out_blocks, forward_way):
    slot_count = tile_values.shape[0]
    feature_width = panels.shape[1]
    panel_blocks = panels.reshape(-1, BLOCK, feature_width)

    def one_slot(slot, totals):
        values = lax.dynamic_index_in_dim(tile_values, slot, 0, keepdims=False)
        source, target = col_index[slot], row_index[slot]
        if not forward_way:
            values, source, target = values.T, target, source
        panel = lax.dynamic_index_in_dim(panel_blocks, source, 0, keepdims=False)
        product = jnp.dot(values, panel, preferred_element_type=jnp.float32)
        return totals.at[target].add(product)

    start = jnp.zeros((out_blocks, BLOCK, feature_width), jnp.float32)
    totals = lax.fori_loop(0, jnp.minimum(live_count, slot_count), one_slot, start)
    return totals.reshape(out_blocks * BLOCK, feature_width)


def slot_device(
    features,
    weight,
    adjacency,
    block_rows,
    block_cols,
    live_blocks,
    part_gains,
    partition,
    cotangent,
):
    node_count = features.shape[0]
    row_total = node_count * lax.axis_size("col") // BLOCK
    col_total = node_count * lax.axis_size("row") // BLOCK
    slots = (adjacency[0, 0], block_rows[0, 0], block_cols[0, 0], live_blocks[0, 0])
    hidden = jnp.dot(features, weight, preferred_element_type=jnp.float32).astype(jnp.bfloat16)
    panels = lax.all_gather(hidden, "row", axis=0, tiled=True)
    member = (
        partition[:, None] == jnp.arange(part_gains.shape[0], dtype=jnp.int32)[None, :]
    ).astype(jnp.float32)
    row_gains = jnp.dot(member, part_gains, precision=lax.Precision.HIGHEST)
    upstream = cotangent.astype(jnp.float32) * row_gains
    partial_rows = slot_sum(*slots, panels, row_total, True)
    summed = lax.psum_scatter(
        partial_rows.astype(jnp.bfloat16), "col", scatter_dimension=0, tiled=True
    ).astype(jnp.float32)
    local_grad = (upstream * silu_slope(summed)).astype(jnp.bfloat16)
    agg_grad = lax.all_gather(local_grad, "col", axis=0, tiled=True)
    activated = jax.nn.silu(summed)
    layer_out = (activated * row_gains).astype(jnp.bfloat16)
    partial_cols = slot_sum(*slots, agg_grad, col_total, False)
    hidden_grad = lax.psum_scatter(
        partial_cols.astype(jnp.bfloat16), "row", scatter_dimension=0, tiled=True
    )
    feature_grad = lax.dot_general(
        hidden_grad, weight, (((1,), (1,)), ((), ())), preferred_element_type=jnp.float32
    ).astype(jnp.bfloat16)
    weight_part = lax.dot_general(
        features, hidden_grad, (((0,), (0,)), ((), ())), preferred_element_type=jnp.float32
    )
    part_terms = jnp.dot(
        member.T, cotangent.astype(jnp.float32) * activated, precision=lax.Precision.HIGHEST
    )
    part_sizes = jnp.sum(member, axis=0)
    weight_total, part_total, size_total = lax.psum(
        (weight_part, part_terms, part_sizes), ("row", "col")
    )
    total_nodes = node_count * lax.axis_size("row") * lax.axis_size("col")
    weight_grad = weight_total / jnp.sqrt(jnp.float32(total_nodes))
    gain_grad = part_total / jnp.sqrt(size_total)[:, None]
    return (layer_out, feature_grad, weight_grad, gain_grad)


def solution(mesh):
    row_count, col_count = mesh.shape["row"], mesh.shape["col"]

    def per_device(features, *others):
        tile_bytes = 2 * features.shape[0] ** 2 * row_count * col_count
        if tile_bytes <= 20 * MIB:
            return dense_device(row_count, col_count, features, *others)
        return slot_device(features, *others)

    in_specs = (
        P(("row", "col"), None),
        P(),
        P("row", "col", None, None, None),
        P("row", "col", None),
        P("row", "col", None),
        P("row", "col"),
        P(),
        P(("row", "col")),
        P(("row", "col"), None),
    )
    out_specs = (P(("row", "col"), None), P(("row", "col"), None), P(), P())
    return jax.shard_map(
        per_device, mesh=mesh, in_specs=in_specs, out_specs=out_specs, check_vma=False
    )
```

```python
import functools
import math

import jax
import jax.numpy as jnp
from jax import lax
from jax.experimental import pallas as pl
from jax.experimental.pallas import tpu as pltpu
from jax.sharding import PartitionSpec as P

BLOCK = 128
GROUP = 16
BUFFERS = 8
HEAVY = 16
CHUNKS = 2
MIB = 1 << 20


def bits_of(count):
    return [1 << b for b in range(count.bit_length() - 1)]


def halving_order(count):
    if count == 1:
        return [0]
    evens = [2 * k for k in halving_order(count // 2)]
    return [k ^ 1 for k in evens] + evens


def build_kernel(
    live_ref, rows_ref, cols_ref, place_row_ref, place_col_ref, slots_ref, tile_ref, buf, total, counts, sems
):
    live = live_ref[0]
    groups = (live + GROUP - 1) // GROUP
    col_blocks = tile_ref.shape[1] // BLOCK

    def fetch(group, slot):
        return pltpu.make_async_copy(
            slots_ref.at[pl.ds(group * GROUP, GROUP)], buf.at[slot], sems.at[slot]
        )

    for b in range(BUFFERS):
        @pl.when(b < groups)
        def _():
            fetch(b, b).start()

    zeros = jnp.zeros((BLOCK, tile_ref.shape[1]), tile_ref.dtype)

    @pl.loop(0, tile_ref.shape[0] // BLOCK)
    def _(r):
        tile_ref[pl.ds(pl.multiple_of(r * BLOCK, BLOCK), BLOCK), :] = zeros

    def place(index):
        top = pl.multiple_of(rows_ref[index] * BLOCK, BLOCK)
        left = pl.multiple_of(cols_ref[index] * BLOCK, BLOCK)
        return pl.ds(top, BLOCK), pl.ds(left, BLOCK)

    @pl.loop(0, groups)
    def _(group):
        slot = lax.rem(group, BUFFERS)
        fetch(group, slot).wait()

        @pl.loop(0, jnp.minimum(GROUP, live - group * GROUP))
        def _(s):
            at = place(group * GROUP + s)
            tile_ref[at] += buf[slot, s]

        @pl.when(group + BUFFERS < groups)
        def _():
            fetch(group + BUFFERS, slot).start()

    slot_total = place_row_ref.shape[1]
    live_here = lax.broadcasted_iota(jnp.int32, (1, slot_total), 1) < live
    same = jnp.where(
        (place_row_ref[...] == place_col_ref[...]) & live_here, 1.0, 0.0
    )
    most = jnp.max(jnp.sum(same, axis=1, keepdims=True))

    @pl.when(most > HEAVY)
    def _():
        @pl.loop(0, counts.shape[0])
        def _(p):
            counts[p] = 0

        @pl.loop(0, live)
        def _(index):
            p = rows_ref[index] * col_blocks + cols_ref[index]
            counts[p] = counts[p] + 1

        @pl.loop(0, live)
        def _(index):
            p = rows_ref[index] * col_blocks + cols_ref[index]

            @pl.when(counts[p] > HEAVY)
            def _():
                counts[p] = 0
                total[...] = jnp.zeros_like(total)

                @pl.loop(index, live)
                def _(other):
                    @pl.when(rows_ref[other] * col_blocks + cols_ref[other] == p)
                    def _():
                        copy = pltpu.make_async_copy(
                            slots_ref.at[pl.ds(other, 1)], buf.at[0, pl.ds(0, 1)], sems.at[0]
                        )
                        copy.start()
                        copy.wait()
                        total[...] += buf[0, 0].astype(jnp.float32)

                tile_ref[place(index)] = total[...].astype(tile_ref.dtype)


def build_tile(slots, rows, cols, live, row_blocks, col_blocks):
    places = rows * col_blocks + cols
    smem = pl.BlockSpec(memory_space=pltpu.SMEM)
    vmem = pl.BlockSpec(memory_space=pltpu.VMEM)
    return pl.pallas_call(
        build_kernel,
        out_shape=pltpu.VMEM((row_blocks * BLOCK, col_blocks * BLOCK), jnp.bfloat16),
        in_specs=[smem, smem, smem, vmem, vmem, pl.BlockSpec(memory_space=pl.ANY)],
        out_specs=vmem,
        scratch_shapes=[
            pltpu.VMEM((BUFFERS, GROUP, BLOCK, BLOCK), jnp.bfloat16),
            pltpu.VMEM((BLOCK, BLOCK), jnp.float32),
            pltpu.SMEM((row_blocks * col_blocks,), jnp.int32),
            pltpu.SemaphoreType.DMA((BUFFERS,)),
        ],
        compiler_params=pltpu.CompilerParams(vmem_limit_bytes=36 * MIB),
        cost_estimate=pl.CostEstimate(flops=0, bytes_accessed=20 * MIB, transcendentals=0),
        name="build_tile",
    )(live, rows, cols, places[None, :], places[:, None], slots)


def forward_kernel(order, chunk, at_ref, tile_ref, *refs):
    *feature_refs, send_ref, rest_ref, panel = refs
    own_row, own_col = at_ref[0], at_ref[1]
    share = feature_refs[0].shape[0]
    for r, feature_ref in enumerate(feature_refs):
        at = pl.ds(pl.multiple_of((own_row ^ r) * share, share), share)
        panel[at, :] = feature_ref[...]
    step = share // CHUNKS
    half = len(order) // 2
    first = chunk * len(order) * step
    for t, k in enumerate(order):
        at = pl.ds(pl.multiple_of(first + (own_col ^ k) * step, step), step)
        product = jnp.dot(tile_ref[at, :], panel[...], preferred_element_type=jnp.float32)
        into = send_ref if t < half else rest_ref
        into[pl.ds((t % half) * step, step), :] = product.astype(jnp.bfloat16)


def forward(chunk, at, tile, features, order):
    share, width = features[0].shape
    part = pltpu.VMEM((len(order) // 2 * share // CHUNKS, width), jnp.bfloat16)
    vmem = pl.BlockSpec(memory_space=pltpu.VMEM)
    smem = pl.BlockSpec(memory_space=pltpu.SMEM)
    return pl.pallas_call(
        functools.partial(forward_kernel, order, chunk),
        out_shape=[part] * 2,
        in_specs=[smem] + [vmem] * (1 + len(features)),
        out_specs=[vmem] * 2,
        scratch_shapes=[pltpu.VMEM((len(features) * share, width), jnp.bfloat16)],
        compiler_params=pltpu.CompilerParams(vmem_limit_bytes=8 * MIB),
        cost_estimate=pl.CostEstimate(
            flops=2 * tile.shape[0] // CHUNKS * tile.shape[1] * width, bytes_accessed=0, transcendentals=0
        ),
        name="forward",
    )(at, tile, *features)


def silu_slope(values):
    sig = jax.nn.sigmoid(values)
    return sig * (1.0 + values * (1.0 - sig))


def wide(values):
    return values.astype(jnp.float32)


def dot_last(left, right):
    return lax.dot_general(left, right, (((1,), (1,)), ((), ())), preferred_element_type=jnp.float32)


def gate_kernel(chunk, upstream_ref, weight_ref, *refs):
    *term_refs, turned_ref, grad_ref, rows_ref, summed_ref = refs
    step = grad_ref.shape[0]
    rows = None
    for term_ref in term_refs:
        term = wide(term_ref[term_ref.shape[0] - step :, :])
        rows = term if rows is None else rows + term
    high = rows.astype(jnp.bfloat16)
    low = (rows - wide(high)).astype(jnp.bfloat16)
    weight = weight_ref[...]
    summed = jnp.dot(high, weight, preferred_element_type=jnp.float32) + jnp.dot(
        low, weight, preferred_element_type=jnp.float32
    )
    upstream = upstream_ref[chunk * step : (chunk + 1) * step, :]
    grad = (upstream * silu_slope(summed)).astype(jnp.bfloat16)
    turned_ref[...] = dot_last(grad, weight).astype(jnp.bfloat16)
    grad_ref[...] = grad
    rows_ref[...] = high
    summed_ref[...] = summed


def gate(chunk, upstream, weight, terms):
    shape = (upstream.shape[0] // CHUNKS, upstream.shape[1])
    vmem = pl.BlockSpec(memory_space=pltpu.VMEM)
    return pl.pallas_call(
        functools.partial(gate_kernel, chunk),
        out_shape=[pltpu.VMEM(shape, jnp.bfloat16)] * 3 + [pltpu.VMEM(shape, jnp.float32)],
        in_specs=[vmem] * (2 + len(terms)),
        out_specs=[vmem] * 4,
        compiler_params=pltpu.CompilerParams(vmem_limit_bytes=8 * MIB),
        cost_estimate=pl.CostEstimate(flops=1 << 27, bytes_accessed=0, transcendentals=1 << 16),
        name="gate",
    )(upstream, weight, *terms)


def pack(values, exact_rows):
    exact = values[values.shape[0] - exact_rows :]
    high = exact.astype(jnp.bfloat16)
    low = (exact - wide(high)).astype(jnp.bfloat16)
    return jnp.concatenate([values[: -exact_rows].astype(jnp.bfloat16), high, low], axis=0)


def unpack(message, exact_rows):
    values = wide(message)
    rows = message.shape[0] - 2 * exact_rows
    exact = values[rows : rows + exact_rows] + values[rows + exact_rows :]
    return jnp.concatenate([values[:rows], exact], axis=0)


def local_kernel(at_ref, members_ref, gains_ref, cotangent_ref, *refs):
    *given, out_ref, keep_ref, send_ref, weights, exact = refs
    step = given[0].shape[0]
    weight_part, part_terms = None, None
    for n in range(CHUNKS):
        rows_ref, grad_ref, summed_ref = given[3 * n : 3 * n + 3]
        at = slice(n * step, (n + 1) * step)
        summed = summed_ref[...]
        activated = summed * jax.nn.sigmoid(summed)
        out_ref[at, :] = (activated * gains_ref[at, :]).astype(out_ref.dtype)
        term = lax.dot_general(
            rows_ref[...], grad_ref[...], (((0,), (0,)), ((), ())), preferred_element_type=jnp.float32
        )
        weight_part = term if weight_part is None else weight_part + term
        term = jnp.dot(
            members_ref[:, at],
            wide(cotangent_ref[at, :]) * activated,
            precision=lax.Precision.HIGHEST,
            preferred_element_type=jnp.float32,
        )
        part_terms = term if part_terms is None else part_terms + term
    weights[...] = weight_part
    count = part_terms.shape[0]
    exact[:count, :] = part_terms
    sizes = jnp.sum(members_ref[...], axis=1, keepdims=True)
    exact[count:, :] = jnp.broadcast_to(sizes, part_terms.shape)
    core = at_ref[1] & 1
    for half, message_ref in ((core, keep_ref), (1 - core, send_ref)):
        rows = weights.shape[0] // 2
        top = weights[pl.ds(pl.multiple_of(half * rows, rows), rows), :]
        bottom = exact[pl.ds(pl.multiple_of(half * count, count), count), :]
        message_ref[...] = pack(jnp.concatenate([top, bottom], axis=0), count)


def local_terms(at, members, gains, cotangent, chunks):
    share, width = cotangent.shape
    count = members.shape[0]
    vmem = pl.BlockSpec(memory_space=pltpu.VMEM)
    smem = pl.BlockSpec(memory_space=pltpu.SMEM)
    given = [x for rows, grad, summed in chunks for x in (rows, grad, summed)]
    return pl.pallas_call(
        local_kernel,
        out_shape=[
            jax.ShapeDtypeStruct((share, width), jnp.bfloat16),
            pltpu.VMEM((width // 2 + 2 * count, width), jnp.bfloat16),
            pltpu.VMEM((width // 2 + 2 * count, width), jnp.bfloat16),
        ],
        in_specs=[smem] + [vmem] * (3 + len(given)),
        out_specs=[vmem] * 3,
        scratch_shapes=[
            pltpu.VMEM((width, width), jnp.float32),
            pltpu.VMEM((2 * count, width), jnp.float32),
        ],
        compiler_params=pltpu.CompilerParams(vmem_limit_bytes=8 * MIB),
        cost_estimate=pl.CostEstimate(flops=1 << 28, bytes_accessed=1 << 19, transcendentals=1 << 17),
        name="local_terms",
    )(at, members, gains, cotangent, *given)


def add_kernel(exact_rows, own_ref, other_ref, out_ref):
    out_ref[...] = pack(
        unpack(own_ref[...], exact_rows) + unpack(other_ref[...], exact_rows), exact_rows
    )


def add_messages(exact_rows, own, other):
    vmem = pl.BlockSpec(memory_space=pltpu.VMEM)
    return pl.pallas_call(
        functools.partial(add_kernel, exact_rows),
        out_shape=pltpu.VMEM(own.shape, jnp.bfloat16),
        in_specs=[vmem] * 2,
        out_specs=vmem,
        compiler_params=pltpu.CompilerParams(vmem_limit_bytes=4 * MIB),
        name="add_messages",
    )(own, other)


def totals_kernel(exact_rows, scale, at_ref, own_ref, other_ref, weight_ref, gain_ref, exact):
    core = at_ref[1] & 1
    rows = weight_ref.shape[0] // 2
    for half, message_ref in ((core, own_ref), (1 - core, other_ref)):
        values = unpack(message_ref[...], exact_rows)
        weight_ref[pl.ds(pl.multiple_of(half * rows, rows), rows), :] = values[:rows] * scale
        exact[pl.ds(pl.multiple_of(half * exact_rows, exact_rows), exact_rows), :] = values[rows:]
    gain_ref[...] = exact[:exact_rows, :] / jnp.sqrt(exact[exact_rows:, :])


def totals(exact_rows, scale, at, own, other):
    width = own.shape[1]
    vmem = pl.BlockSpec(memory_space=pltpu.VMEM)
    smem = pl.BlockSpec(memory_space=pltpu.SMEM)
    return pl.pallas_call(
        functools.partial(totals_kernel, exact_rows, scale),
        out_shape=[
            jax.ShapeDtypeStruct((width, width), jnp.float32),
            jax.ShapeDtypeStruct((exact_rows, width), jnp.float32),
        ],
        in_specs=[smem] + [vmem] * 2,
        out_specs=[vmem] * 2,
        scratch_shapes=[pltpu.VMEM((2 * exact_rows, width), jnp.float32)],
        compiler_params=pltpu.CompilerParams(vmem_limit_bytes=4 * MIB),
        name="totals",
    )(at, own, other)


def backward_kernel(orders, row_count, chunk, at_ref, tile_ref, *refs):
    grad_refs, refs = refs[: len(orders)], refs[len(orders) :]
    before_refs, refs = refs[: row_count * (chunk > 0)], refs[row_count * (chunk > 0) :]
    *part_refs, turned = refs
    own_row, own_col = at_ref[0], at_ref[1]
    step = turned.shape[1] // sum(len(o) for o in orders)
    for order, grad_ref in zip(orders, grad_refs):
        for t, k in enumerate(order):
            at = pl.ds(pl.multiple_of((own_col ^ k) * step, step), step)
            turned[:, at] = grad_ref[t * step : (t + 1) * step, :].T
    share = part_refs[0].shape[1]
    depth = turned.shape[1]
    for r in reversed(range(row_count)):
        at = pl.ds(pl.multiple_of((own_row ^ r) * share, share), share)
        product = jnp.dot(
            turned[...],
            tile_ref[chunk * depth : (chunk + 1) * depth, at],
            preferred_element_type=jnp.float32,
        )
        if chunk:
            product = product + before_refs[r][...]
        part_refs[r][...] = product.astype(part_refs[r].dtype)


def backward(chunk, at, tile, grads, orders, before, share, row_count):
    width = grads[0].shape[1]
    last = chunk == CHUNKS - 1
    vmem = pl.BlockSpec(memory_space=pltpu.VMEM)
    smem = pl.BlockSpec(memory_space=pltpu.SMEM)
    kinds = [jnp.bfloat16 if last and r else jnp.float32 for r in range(row_count)]
    return pl.pallas_call(
        functools.partial(backward_kernel, orders, row_count, chunk),
        out_shape=[pltpu.VMEM((width, share), kind) for kind in kinds],
        in_specs=[smem] + [vmem] * (1 + len(grads) + len(before)),
        out_specs=[vmem] * row_count,
        scratch_shapes=[pltpu.VMEM((width, tile.shape[0] // CHUNKS), jnp.bfloat16)],
        compiler_params=pltpu.CompilerParams(vmem_limit_bytes=8 * MIB),
        cost_estimate=pl.CostEstimate(
            flops=2 * tile.shape[0] // CHUNKS * tile.shape[1] * width, bytes_accessed=0, transcendentals=0
        ),
        name="backward",
    )(at, tile, *grads, *before)


def finish_kernel(*refs):
    *part_refs, out_ref = refs
    total = None
    for part_ref in part_refs:
        term = wide(part_ref[...])
        total = term if total is None else total + term
    out_ref[...] = total.T.astype(out_ref.dtype)


def finish(parts):
    width, share = parts[0].shape
    vmem = pl.BlockSpec(memory_space=pltpu.VMEM)
    return pl.pallas_call(
        finish_kernel,
        out_shape=jax.ShapeDtypeStruct((share, width), jnp.bfloat16),
        in_specs=[vmem] * len(parts),
        out_specs=vmem,
        compiler_params=pltpu.CompilerParams(vmem_limit_bytes=8 * MIB),
        name="finish",
    )(*parts)


def swap(values, axis, mask, count):
    return lax.ppermute(values, axis, [(d, d ^ mask) for d in range(count)])


def after(values, *others):
    return lax.optimization_barrier((values, *others))[0]


def dense_device(
    row_count,
    col_count,
    features,
    weight,
    adjacency,
    block_rows,
    block_cols,
    live_blocks,
    part_gains,
    partition,
    cotangent,
):
    share, width = features.shape
    step = share // CHUNKS
    row_blocks = share * col_count // BLOCK
    at = jnp.stack([lax.axis_index("row"), lax.axis_index("col")]).astype(jnp.int32)
    gathered = [features] + [swap(features, "row", r, row_count) for r in range(1, row_count)]
    per_device, per_chunk = share // BLOCK, step // BLOCK
    rows, cols = block_rows[0, 0], block_cols[0, 0]
    owner, inner = rows // per_device, rows % per_device
    rows = (inner // per_chunk * col_count + owner) * per_chunk + inner % per_chunk
    tile = build_tile(
        adjacency[0, 0], rows, cols, live_blocks[0], row_blocks, share * row_count // BLOCK
    )
    part_count = part_gains.shape[0]
    members = (
        partition[None, :] == jnp.arange(part_count, dtype=jnp.int32)[:, None]
    ).astype(jnp.float32)
    row_gains = lax.dot_general(
        members, part_gains, (((0,), (0,)), ((), ())), precision=lax.Precision.HIGHEST
    )
    upstream = wide(cotangent) * row_gains

    order = halving_order(col_count)
    col_bits = bits_of(col_count)
    chunks = range(CHUNKS)
    sends, rests = zip(*(forward(n, at, tile, gathered, order) for n in chunks))
    sends, rests = list(sends), list(rests)

    arrived = [[swap(send, "col", col_bits[0], col_count)] for send in sends]
    for bit in col_bits[1:]:
        last = None
        for n in chunks:
            rest = rests[n]
            half = rest.shape[0] // 2
            first = sum(wide(a[-2 * half :][:half]) for a in arrived[n])
            out = (wide(rest[:half]) + first).astype(jnp.bfloat16)
            if last is not None:
                out = after(out, last)
            last = out
            arrived[n].append(swap(out, "col", bit, col_count))
            rests[n] = rest[half:]
    gated = []
    for n in chunks:
        up = after(upstream, gated[-1][0]) if n else upstream
        gated.append(gate(n, up, weight, [rests[n]] + arrived[n]))
    held, orders = [[g[0]] for g in gated], [[0]]
    for bit in reversed(col_bits[1:]):
        last = None
        for n in chunks:
            sent = held[n][0] if len(orders) == 1 else jnp.concatenate(held[n][::-1], axis=0)
            if last is not None:
                sent = after(sent, last)
            last = sent
            held[n].append(swap(sent, "col", bit, col_count))
        orders.append([k ^ bit for o in orders[::-1] for k in o])

    layer_out, message, out = local_terms(
        at, members, row_gains, cotangent, [(rows, grad, summed) for _, grad, rows, summed in gated]
    )
    stages = [("col", col_bits[0], col_count)]
    stages += [("row", bit, row_count) for bit in bits_of(row_count)]
    stages += [("col", bit, col_count) for bit in col_bits[1:]]
    for stage in stages:
        message = add_messages(part_count, message, swap(out, *stage))
        out = message
    other = swap(message, "col", col_bits[0], col_count)
    scale = 1.0 / math.sqrt(share * row_count * col_count)
    weight_grad, gain_grad = totals(part_count, scale, at, message, other)

    parts = []
    bit = col_bits[0]
    piece_orders = orders + [[k ^ bit for k in o] for o in orders]
    for n in chunks:
        pieces = held[n] + [swap(h, "col", bit, col_count) for h in held[n]]
        parts = backward(n, at, tile, pieces, piece_orders, parts, share, row_count)
    parts = [p if r == 0 else swap(p, "row", r, row_count) for r, p in enumerate(parts)]
    feature_grad = finish(parts)

    return (layer_out, feature_grad, weight_grad, gain_grad)


def slot_sum(tile_values, row_index, col_index, live_count, panels, out_blocks, forward_way):
    slot_count = tile_values.shape[0]
    feature_width = panels.shape[1]
    panel_blocks = panels.reshape(-1, BLOCK, feature_width)

    def one_slot(slot, totals):
        values = lax.dynamic_index_in_dim(tile_values, slot, 0, keepdims=False)
        source, target = col_index[slot], row_index[slot]
        if not forward_way:
            values, source, target = values.T, target, source
        panel = lax.dynamic_index_in_dim(panel_blocks, source, 0, keepdims=False)
        product = jnp.dot(values, panel, preferred_element_type=jnp.float32)
        return totals.at[target].add(product)

    start = jnp.zeros((out_blocks, BLOCK, feature_width), jnp.float32)
    totals = lax.fori_loop(0, jnp.minimum(live_count, slot_count), one_slot, start)
    return totals.reshape(out_blocks * BLOCK, feature_width)


def slot_device(
    features,
    weight,
    adjacency,
    block_rows,
    block_cols,
    live_blocks,
    part_gains,
    partition,
    cotangent,
):
    node_count = features.shape[0]
    row_total = node_count * lax.axis_size("col") // BLOCK
    col_total = node_count * lax.axis_size("row") // BLOCK
    slots = (adjacency[0, 0], block_rows[0, 0], block_cols[0, 0], live_blocks[0, 0])
    hidden = jnp.dot(features, weight, preferred_element_type=jnp.float32).astype(jnp.bfloat16)
    panels = lax.all_gather(hidden, "row", axis=0, tiled=True)
    member = (
        partition[:, None] == jnp.arange(part_gains.shape[0], dtype=jnp.int32)[None, :]
    ).astype(jnp.float32)
    row_gains = jnp.dot(member, part_gains, precision=lax.Precision.HIGHEST)
    upstream = cotangent.astype(jnp.float32) * row_gains
    partial_rows = slot_sum(*slots, panels, row_total, True)
    summed = lax.psum_scatter(
        partial_rows.astype(jnp.bfloat16), "col", scatter_dimension=0, tiled=True
    ).astype(jnp.float32)
    local_grad = (upstream * silu_slope(summed)).astype(jnp.bfloat16)
    agg_grad = lax.all_gather(local_grad, "col", axis=0, tiled=True)
    activated = jax.nn.silu(summed)
    layer_out = (activated * row_gains).astype(jnp.bfloat16)
    partial_cols = slot_sum(*slots, agg_grad, col_total, False)
    hidden_grad = lax.psum_scatter(
        partial_cols.astype(jnp.bfloat16), "row", scatter_dimension=0, tiled=True
    )
    feature_grad = lax.dot_general(
        hidden_grad, weight, (((1,), (1,)), ((), ())), preferred_element_type=jnp.float32
    ).astype(jnp.bfloat16)
    weight_part = lax.dot_general(
        features, hidden_grad, (((0,), (0,)), ((), ())), preferred_element_type=jnp.float32
    )
    part_terms = jnp.dot(
        member.T, cotangent.astype(jnp.float32) * activated, precision=lax.Precision.HIGHEST
    )
    part_sizes = jnp.sum(member, axis=0)
    weight_total, part_total, size_total = lax.psum(
        (weight_part, part_terms, part_sizes), ("row", "col")
    )
    total_nodes = node_count * lax.axis_size("row") * lax.axis_size("col")
    weight_grad = weight_total / jnp.sqrt(jnp.float32(total_nodes))
    gain_grad = part_total / jnp.sqrt(size_total)[:, None]
    return (layer_out, feature_grad, weight_grad, gain_grad)


def solution(mesh):
    row_count, col_count = mesh.shape["row"], mesh.shape["col"]

    def per_device(features, *others):
        tile_bytes = 2 * features.shape[0] ** 2 * row_count * col_count
        if tile_bytes <= 20 * MIB:
            return dense_device(row_count, col_count, features, *others)
        return slot_device(features, *others)

    in_specs = (
        P(("row", "col"), None),
        P(),
        P("row", "col", None, None, None),
        P("row", "col", None),
        P("row", "col", None),
        P("row", "col"),
        P(),
        P(("row", "col")),
        P(("row", "col"), None),
    )
    out_specs = (P(("row", "col"), None), P(("row", "col"), None), P(), P())
    return jax.shard_map(
        per_device, mesh=mesh, in_specs=in_specs, out_specs=out_specs, check_vma=False
    )
```

```python
import functools
import math

import jax
import jax.numpy as jnp
from jax import lax
from jax.experimental import pallas as pl
from jax.experimental.pallas import tpu as pltpu
from jax.sharding import PartitionSpec as P

BLOCK = 128
GROUP = 16
BUFFERS = 8
HEAVY = 16
CHUNKS = 2
MIB = 1 << 20
LIGHT = pl.CostEstimate(flops=1, bytes_accessed=1, transcendentals=0)


def bits_of(count):
    return [1 << b for b in range(count.bit_length() - 1)]


def halving_order(count):
    if count == 1:
        return [0]
    evens = [2 * k for k in halving_order(count // 2)]
    return [k ^ 1 for k in evens] + evens


def shift_of(count):
    return count.bit_length() - 1


def build_kernel(
    layout, live_ref, rows_ref, cols_ref, row_lane_ref, col_lane_ref, slots_ref, tile_ref, buf, total, counts, sems
):
    owners, per_owner, per_chunk = layout
    live = live_ref[0, 0]
    groups = (live + GROUP - 1) // GROUP
    col_blocks = tile_ref.shape[1] // BLOCK

    def fetch(group, slot):
        return pltpu.make_async_copy(
            slots_ref.at[0, 0, pl.ds(group * GROUP, GROUP)], buf.at[slot], sems.at[slot]
        )

    for b in range(BUFFERS):
        @pl.when(b < groups)
        def _():
            fetch(b, b).start()

    zeros = jnp.zeros((BLOCK, tile_ref.shape[1]), tile_ref.dtype)

    @pl.loop(0, tile_ref.shape[0] // BLOCK)
    def _(r):
        tile_ref[pl.ds(pl.multiple_of(r * BLOCK, BLOCK), BLOCK), :] = zeros

    lane_places = row_lane_ref[0] * col_blocks + col_lane_ref[0]
    slot_total = lane_places.shape[1]
    places = jnp.broadcast_to(lane_places.astype(jnp.float32), (BLOCK, slot_total))
    live_lanes = lax.broadcasted_iota(jnp.int32, (1, slot_total), 1) < live
    same = jnp.where((places.T[:, :1] == places[:1, :]) & live_lanes, 1.0, 0.0)
    most = jnp.max(jnp.sum(same, axis=1, keepdims=True))

    def place(index):
        row = rows_ref[0, 0, index]
        owner, inner = row >> shift_of(per_owner), row & (per_owner - 1)
        chunk, inner = inner >> shift_of(per_chunk), inner & (per_chunk - 1)
        row = (chunk * owners + owner) * per_chunk + inner
        top = pl.multiple_of(row * BLOCK, BLOCK)
        left = pl.multiple_of(cols_ref[0, 0, index] * BLOCK, BLOCK)
        return pl.ds(top, BLOCK), pl.ds(left, BLOCK)

    @pl.loop(0, groups)
    def _(group):
        slot = lax.rem(group, BUFFERS)
        fetch(group, slot).wait()

        def add(s):
            at = place(group * GROUP + s)
            tile_ref[at] += buf[slot, s]

        here = live - group * GROUP

        @pl.when(here >= GROUP)
        def _():
            for s in range(GROUP):
                add(s)

        @pl.when(here < GROUP)
        def _():
            pl.loop(0, here)(add)

        @pl.when(group + BUFFERS < groups)
        def _():
            fetch(group + BUFFERS, slot).start()

    @pl.when(most > HEAVY)
    def _():
        @pl.loop(0, counts.shape[0])
        def _(p):
            counts[p] = 0

        @pl.loop(0, live)
        def _(index):
            p = rows_ref[0, 0, index] * col_blocks + cols_ref[0, 0, index]
            counts[p] = counts[p] + 1

        @pl.loop(0, live)
        def _(index):
            p = rows_ref[0, 0, index] * col_blocks + cols_ref[0, 0, index]

            @pl.when(counts[p] > HEAVY)
            def _():
                counts[p] = 0
                total[...] = jnp.zeros_like(total)

                @pl.loop(index, live)
                def _(other):
                    @pl.when(rows_ref[0, 0, other] * col_blocks + cols_ref[0, 0, other] == p)
                    def _():
                        copy = pltpu.make_async_copy(
                            slots_ref.at[0, 0, pl.ds(other, 1)], buf.at[0, pl.ds(0, 1)], sems.at[0]
                        )
                        copy.start()
                        copy.wait()
                        total[...] += buf[0, 0].astype(jnp.float32)

                tile_ref[place(index)] = total[...].astype(tile_ref.dtype)


def build_tile(slots, rows, cols, live, row_blocks, col_blocks, layout):
    smem = pl.BlockSpec(memory_space=pltpu.SMEM)
    vmem = pl.BlockSpec(memory_space=pltpu.VMEM)
    return pl.pallas_call(
        functools.partial(build_kernel, layout),
        out_shape=pltpu.VMEM((row_blocks * BLOCK, col_blocks * BLOCK), jnp.bfloat16),
        in_specs=[smem, smem, smem, vmem, vmem, pl.BlockSpec(memory_space=pl.ANY)],
        out_specs=vmem,
        scratch_shapes=[
            pltpu.VMEM((BUFFERS, GROUP, BLOCK, BLOCK), jnp.bfloat16),
            pltpu.VMEM((BLOCK, BLOCK), jnp.float32),
            pltpu.SMEM((row_blocks * col_blocks,), jnp.int32),
            pltpu.SemaphoreType.DMA((BUFFERS,)),
        ],
        compiler_params=pltpu.CompilerParams(vmem_limit_bytes=36 * MIB),
        cost_estimate=pl.CostEstimate(flops=0, bytes_accessed=20 * MIB, transcendentals=0),
        name="build_tile",
    )(live, rows, cols, rows, cols, slots)


def forward_kernel(order, chunk, at_ref, tile_ref, *refs):
    *feature_refs, send_ref, rest_ref, panel = refs
    own_row, own_col = at_ref[0], at_ref[1]
    share = feature_refs[0].shape[0]
    for r, feature_ref in enumerate(feature_refs):
        at = pl.ds(pl.multiple_of((own_row ^ r) * share, share), share)
        panel[at, :] = feature_ref[...]
    step = share // CHUNKS
    half = len(order) // 2
    first = chunk * len(order) * step
    for t, k in enumerate(order):
        at = pl.ds(pl.multiple_of(first + (own_col ^ k) * step, step), step)
        product = jnp.dot(tile_ref[at, :], panel[...], preferred_element_type=jnp.float32)
        into = send_ref if t < half else rest_ref
        into[pl.ds((t % half) * step, step), :] = product.astype(jnp.bfloat16)


def forward(chunk, at, tile, features, order):
    share, width = features[0].shape
    part = pltpu.VMEM((len(order) // 2 * share // CHUNKS, width), jnp.bfloat16)
    vmem = pl.BlockSpec(memory_space=pltpu.VMEM)
    smem = pl.BlockSpec(memory_space=pltpu.SMEM)
    return pl.pallas_call(
        functools.partial(forward_kernel, order, chunk),
        out_shape=[part] * 2,
        in_specs=[smem] + [vmem] * (1 + len(features)),
        out_specs=[vmem] * 2,
        scratch_shapes=[pltpu.VMEM((len(features) * share, width), jnp.bfloat16)],
        compiler_params=pltpu.CompilerParams(vmem_limit_bytes=8 * MIB),
        cost_estimate=pl.CostEstimate(
            flops=2 * tile.shape[0] // CHUNKS * tile.shape[1] * width, bytes_accessed=0, transcendentals=0
        ),
        name="forward",
    )(at, tile, *features)


def silu_slope(values):
    sig = jax.nn.sigmoid(values)
    return sig * (1.0 + values * (1.0 - sig))


def wide(values):
    return values.astype(jnp.float32)


def dot_last(left, right):
    return lax.dot_general(left, right, (((1,), (1,)), ((), ())), preferred_element_type=jnp.float32)


def combine_kernel(specs, *refs):
    out_refs = refs[-len(specs) :]
    for spec, out_ref in zip(specs, out_refs):
        total = None
        for source, start in spec:
            term = wide(refs[source][start : start + out_ref.shape[0], :])
            total = term if total is None else total + term
        out_ref[...] = total.astype(out_ref.dtype)


def combine(step, sums):
    sources = list({id(x): x for terms in sums for x, _ in terms}.values())
    at = {id(x): i for i, x in enumerate(sources)}
    specs = [[(at[id(x)], start) for x, start in terms] for terms in sums]
    vmem = pl.BlockSpec(memory_space=pltpu.VMEM)
    return pl.pallas_call(
        functools.partial(combine_kernel, specs),
        out_shape=[pltpu.VMEM((step, sources[0].shape[1]), jnp.bfloat16)] * len(sums),
        in_specs=[vmem] * len(sources),
        out_specs=[vmem] * len(sums),
        compiler_params=pltpu.CompilerParams(vmem_limit_bytes=4 * MIB),
        cost_estimate=LIGHT,
        name="combine",
    )(*sources)


def gate_kernel(chunk, starts, upstream_ref, weight_ref, *refs):
    *term_refs, turned_ref, grad_ref, rows_ref, summed_ref = refs
    step = grad_ref.shape[0]
    rows = None
    for term_ref, start in zip(term_refs, starts):
        term = wide(term_ref[start : start + step, :])
        rows = term if rows is None else rows + term
    high = rows.astype(jnp.bfloat16)
    low = (rows - wide(high)).astype(jnp.bfloat16)
    weight = weight_ref[...]
    summed = jnp.dot(high, weight, preferred_element_type=jnp.float32) + jnp.dot(
        low, weight, preferred_element_type=jnp.float32
    )
    upstream = upstream_ref[chunk * step : (chunk + 1) * step, :]
    grad = (upstream * silu_slope(summed)).astype(jnp.bfloat16)
    turned_ref[...] = dot_last(grad, weight).astype(jnp.bfloat16)
    grad_ref[...] = grad
    rows_ref[...] = high
    summed_ref[...] = summed


def gate(chunk, upstream, weight, terms):
    shape = (upstream.shape[0] // CHUNKS, upstream.shape[1])
    vmem = pl.BlockSpec(memory_space=pltpu.VMEM)
    return pl.pallas_call(
        functools.partial(gate_kernel, chunk, [start for _, start in terms]),
        out_shape=[pltpu.VMEM(shape, jnp.bfloat16)] * 3 + [pltpu.VMEM(shape, jnp.float32)],
        in_specs=[vmem] * (2 + len(terms)),
        out_specs=[vmem] * 4,
        compiler_params=pltpu.CompilerParams(vmem_limit_bytes=8 * MIB),
        cost_estimate=LIGHT,
        name="gate",
    )(upstream, weight, *(x for x, _ in terms))


def pack(values, exact_rows):
    exact = values[values.shape[0] - exact_rows :]
    high = exact.astype(jnp.bfloat16)
    low = (exact - wide(high)).astype(jnp.bfloat16)
    return jnp.concatenate([values[: -exact_rows].astype(jnp.bfloat16), high, low], axis=0)


def unpack(message, exact_rows):
    values = wide(message)
    rows = message.shape[0] - 2 * exact_rows
    exact = values[rows : rows + exact_rows] + values[rows + exact_rows :]
    return jnp.concatenate([values[:rows], exact], axis=0)


def local_kernel(at_ref, members_ref, gains_ref, cotangent_ref, *refs):
    *given, out_ref, keep_ref, send_ref, weights, exact = refs
    step = given[0].shape[0]
    weight_part, part_terms = None, None
    for n in range(CHUNKS):
        rows_ref, grad_ref, summed_ref = given[3 * n : 3 * n + 3]
        at = slice(n * step, (n + 1) * step)
        summed = summed_ref[...]
        activated = summed * jax.nn.sigmoid(summed)
        out_ref[at, :] = (activated * gains_ref[at, :]).astype(out_ref.dtype)
        term = lax.dot_general(
            rows_ref[...], grad_ref[...], (((0,), (0,)), ((), ())), preferred_element_type=jnp.float32
        )
        weight_part = term if weight_part is None else weight_part + term
        term = jnp.dot(
            members_ref[:, at],
            wide(cotangent_ref[at, :]) * activated,
            precision=lax.Precision.HIGHEST,
            preferred_element_type=jnp.float32,
        )
        part_terms = term if part_terms is None else part_terms + term
    weights[...] = weight_part
    count = part_terms.shape[0]
    exact[:count, :] = part_terms
    sizes = jnp.sum(members_ref[...], axis=1, keepdims=True)
    exact[count:, :] = jnp.broadcast_to(sizes, part_terms.shape)
    core = at_ref[1] & 1
    for half, message_ref in ((core, keep_ref), (1 - core, send_ref)):
        rows = weights.shape[0] // 2
        top = weights[pl.ds(pl.multiple_of(half * rows, rows), rows), :]
        bottom = exact[pl.ds(pl.multiple_of(half * count, count), count), :]
        message_ref[...] = pack(jnp.concatenate([top, bottom], axis=0), count)


def local_terms(at, members, gains, cotangent, chunks):
    share, width = cotangent.shape
    count = members.shape[0]
    vmem = pl.BlockSpec(memory_space=pltpu.VMEM)
    smem = pl.BlockSpec(memory_space=pltpu.SMEM)
    given = [x for rows, grad, summed in chunks for x in (rows, grad, summed)]
    return pl.pallas_call(
        local_kernel,
        out_shape=[
            jax.ShapeDtypeStruct((share, width), jnp.bfloat16),
            pltpu.VMEM((width // 2 + 2 * count, width), jnp.bfloat16),
            pltpu.VMEM((width // 2 + 2 * count, width), jnp.bfloat16),
        ],
        in_specs=[smem] + [vmem] * (3 + len(given)),
        out_specs=[vmem] * 3,
        scratch_shapes=[
            pltpu.VMEM((width, width), jnp.float32),
            pltpu.VMEM((2 * count, width), jnp.float32),
        ],
        compiler_params=pltpu.CompilerParams(vmem_limit_bytes=8 * MIB),
        cost_estimate=LIGHT,
        name="local_terms",
    )(at, members, gains, cotangent, *given)


def add_kernel(exact_rows, own_ref, other_ref, out_ref):
    out_ref[...] = pack(
        unpack(own_ref[...], exact_rows) + unpack(other_ref[...], exact_rows), exact_rows
    )


def add_messages(exact_rows, own, other):
    vmem = pl.BlockSpec(memory_space=pltpu.VMEM)
    return pl.pallas_call(
        functools.partial(add_kernel, exact_rows),
        out_shape=pltpu.VMEM(own.shape, jnp.bfloat16),
        in_specs=[vmem] * 2,
        out_specs=vmem,
        compiler_params=pltpu.CompilerParams(vmem_limit_bytes=4 * MIB),
        cost_estimate=LIGHT,
        name="add_messages",
    )(own, other)


def totals_kernel(exact_rows, scale, at_ref, own_ref, other_ref, weight_ref, gain_ref, exact):
    core = at_ref[1] & 1
    rows = weight_ref.shape[0] // 2
    for half, message_ref in ((core, own_ref), (1 - core, other_ref)):
        values = unpack(message_ref[...], exact_rows)
        weight_ref[pl.ds(pl.multiple_of(half * rows, rows), rows), :] = values[:rows] * scale
        exact[pl.ds(pl.multiple_of(half * exact_rows, exact_rows), exact_rows), :] = values[rows:]
    gain_ref[...] = exact[:exact_rows, :] / jnp.sqrt(exact[exact_rows:, :])


def totals(exact_rows, scale, at, own, other):
    width = own.shape[1]
    vmem = pl.BlockSpec(memory_space=pltpu.VMEM)
    smem = pl.BlockSpec(memory_space=pltpu.SMEM)
    return pl.pallas_call(
        functools.partial(totals_kernel, exact_rows, scale),
        out_shape=[
            jax.ShapeDtypeStruct((width, width), jnp.float32),
            jax.ShapeDtypeStruct((exact_rows, width), jnp.float32),
        ],
        in_specs=[smem] + [vmem] * 2,
        out_specs=[vmem] * 2,
        scratch_shapes=[pltpu.VMEM((2 * exact_rows, width), jnp.float32)],
        compiler_params=pltpu.CompilerParams(vmem_limit_bytes=4 * MIB),
        cost_estimate=LIGHT,
        name="totals",
    )(at, own, other)


def backward_kernel(orders, row_count, chunk, at_ref, tile_ref, *refs):
    grad_refs, refs = refs[: len(orders)], refs[len(orders) :]
    before_refs, refs = refs[: row_count * (chunk > 0)], refs[row_count * (chunk > 0) :]
    *part_refs, turned = refs
    own_row, own_col = at_ref[0], at_ref[1]
    step = grad_refs[0].shape[0]
    for order, grad_ref in zip(orders, grad_refs):
        for t, k in enumerate(order):
            at = pl.ds(pl.multiple_of((own_col ^ k) * step, step), step)
            turned[:, at] = grad_ref[t * step : (t + 1) * step, :].T
    share = part_refs[0].shape[1]
    depth = turned.shape[1]
    for r in reversed(range(row_count)):
        at = pl.ds(pl.multiple_of((own_row ^ r) * share, share), share)
        product = jnp.dot(
            turned[...],
            tile_ref[chunk * depth : (chunk + 1) * depth, at],
            preferred_element_type=jnp.float32,
        )
        if chunk:
            product = product + before_refs[r][...]
        part_refs[r][...] = product.astype(part_refs[r].dtype)


def backward(chunk, at, tile, grads, orders, before, share, row_count):
    width = grads[0].shape[1]
    last = chunk == CHUNKS - 1
    vmem = pl.BlockSpec(memory_space=pltpu.VMEM)
    smem = pl.BlockSpec(memory_space=pltpu.SMEM)
    kinds = [jnp.bfloat16 if last and r else jnp.float32 for r in range(row_count)]
    return pl.pallas_call(
        functools.partial(backward_kernel, orders, row_count, chunk),
        out_shape=[pltpu.VMEM((width, share), kind) for kind in kinds],
        in_specs=[smem] + [vmem] * (1 + len(grads) + len(before)),
        out_specs=[vmem] * row_count,
        scratch_shapes=[pltpu.VMEM((width, tile.shape[0] // CHUNKS), jnp.bfloat16)],
        compiler_params=pltpu.CompilerParams(vmem_limit_bytes=8 * MIB),
        cost_estimate=pl.CostEstimate(
            flops=tile.shape[0] // CHUNKS * tile.shape[1] * width, bytes_accessed=0, transcendentals=0
        ),
        name="backward",
    )(at, tile, *grads, *before)


def finish_kernel(*refs):
    *part_refs, out_ref = refs
    total = None
    for part_ref in part_refs:
        term = wide(part_ref[...])
        total = term if total is None else total + term
    out_ref[...] = total.T.astype(out_ref.dtype)


def finish(parts):
    width, share = parts[0].shape
    vmem = pl.BlockSpec(memory_space=pltpu.VMEM)
    return pl.pallas_call(
        finish_kernel,
        out_shape=jax.ShapeDtypeStruct((share, width), jnp.bfloat16),
        in_specs=[vmem] * len(parts),
        out_specs=vmem,
        compiler_params=pltpu.CompilerParams(vmem_limit_bytes=8 * MIB),
        cost_estimate=LIGHT,
        name="finish",
    )(*parts)


def swap(values, axis, mask, count):
    return lax.ppermute(values, axis, [(d, d ^ mask) for d in range(count)])


def after(values, *others):
    return lax.optimization_barrier((values, *others))[0]


def dense_device(
    row_count,
    col_count,
    features,
    weight,
    adjacency,
    block_rows,
    block_cols,
    live_blocks,
    part_gains,
    partition,
    cotangent,
):
    share, width = features.shape
    step = share // CHUNKS
    row_blocks = share * col_count // BLOCK
    at = jnp.stack([lax.axis_index("row"), lax.axis_index("col")]).astype(jnp.int32)
    gathered = [features] + [swap(features, "row", r, row_count) for r in range(1, row_count)]
    layout = (col_count, share // BLOCK, step // BLOCK)
    tile = build_tile(
        adjacency, block_rows, block_cols, live_blocks, row_blocks, share * row_count // BLOCK, layout
    )
    part_count = part_gains.shape[0]
    members = (
        partition[None, :] == jnp.arange(part_count, dtype=jnp.int32)[:, None]
    ).astype(jnp.float32)
    row_gains = lax.dot_general(
        members, part_gains, (((0,), (0,)), ((), ())), precision=lax.Precision.HIGHEST
    )
    upstream = wide(cotangent) * row_gains

    order = halving_order(col_count)
    col_bits = bits_of(col_count)
    chunks = range(CHUNKS)
    sends, rests = zip(*(forward(n, at, tile, gathered, order) for n in chunks))
    sends, rests = list(sends), list(rests)

    pending = []
    for n in chunks:
        other = swap(sends[n], "col", col_bits[0], col_count)
        kept = enumerate(order[len(order) // 2 :])
        pending.append({k: [(rests[n], t * step), (other, t * step)] for t, k in kept})
    last = None
    for bit in col_bits[1:]:
        for terms in pending:
            blocks = sorted((k for k in terms if k & bit), reverse=True)
            sums = [terms.pop(k) for k in blocks]
            if last is not None:
                x, start = sums[0][-1]
                sums[0][-1] = (after(x, last), start)
            outs = combine(step, sums)
            last = outs[0]
            for k, out in zip(blocks, outs):
                terms[k ^ bit].append((swap(out, "col", bit, col_count), 0))
    gated, held = [], []
    for n in chunks:
        gated.append(gate(n, after(upstream, last), weight, pending[n][0]))
        last = gated[-1][0]
        held.append({0: last})
    scale = 1.0 / math.sqrt(share * row_count * col_count)
    messages = []
    for bit in reversed(col_bits[1:]):
        for n in chunks:
            for k in list(held[n]):
                sent = held[n][k]
                if k and n == 0:
                    sent = last = after(sent, last)
                if k and n:
                    if not messages:
                        ready = after(at, last)
                        local = [(rows, grad, summed) for _, grad, rows, summed in gated]
                        layer_out, message, out = local_terms(
                            ready, members, row_gains, cotangent, local
                        )
                        message = add_messages(
                            part_count, message, swap(out, "col", col_bits[0], col_count)
                        )
                        messages.append(message)
                    sent = after(sent, messages[0], *held[n].values())
                held[n][k ^ bit] = swap(sent, "col", bit, col_count)
    stages = [("row", bit, row_count) for bit in bits_of(row_count)]
    stages += [("col", bit, col_count) for bit in col_bits[1:]]
    for stage in stages:
        message = add_messages(part_count, message, swap(message, *stage))
        messages.append(message)
    other = swap(message, "col", col_bits[0], col_count)
    weight_grad, gain_grad = totals(part_count, scale, at, message, other)

    parts = []
    bit = col_bits[0]
    for n in chunks:
        sent = jnp.concatenate(list(held[n].values()), axis=0)
        if n:
            sent = after(sent, messages[1])
        pieces = list(held[n].values()) + [swap(sent, "col", bit, col_count)]
        piece_orders = [[k] for k in held[n]] + [[k ^ bit for k in held[n]]]
        parts = backward(n, at, tile, pieces, piece_orders, parts, share, row_count)
    parts = [p if r == 0 else swap(p, "row", r, row_count) for r, p in enumerate(parts)]
    feature_grad = finish(parts)

    return (layer_out, feature_grad, weight_grad, gain_grad)


def slot_sum(tile_values, row_index, col_index, live_count, panels, out_blocks, forward_way):
    slot_count = tile_values.shape[0]
    feature_width = panels.shape[1]
    panel_blocks = panels.reshape(-1, BLOCK, feature_width)

    def one_slot(slot, totals):
        values = lax.dynamic_index_in_dim(tile_values, slot, 0, keepdims=False)
        source, target = col_index[slot], row_index[slot]
        if not forward_way:
            values, source, target = values.T, target, source
        panel = lax.dynamic_index_in_dim(panel_blocks, source, 0, keepdims=False)
        product = jnp.dot(values, panel, preferred_element_type=jnp.float32)
        return totals.at[target].add(product)

    start = jnp.zeros((out_blocks, BLOCK, feature_width), jnp.float32)
    totals = lax.fori_loop(0, jnp.minimum(live_count, slot_count), one_slot, start)
    return totals.reshape(out_blocks * BLOCK, feature_width)


def slot_device(
    features,
    weight,
    adjacency,
    block_rows,
    block_cols,
    live_blocks,
    part_gains,
    partition,
    cotangent,
):
    node_count = features.shape[0]
    row_total = node_count * lax.axis_size("col") // BLOCK
    col_total = node_count * lax.axis_size("row") // BLOCK
    slots = (adjacency[0, 0], block_rows[0, 0], block_cols[0, 0], live_blocks[0, 0])
    hidden = jnp.dot(features, weight, preferred_element_type=jnp.float32).astype(jnp.bfloat16)
    panels = lax.all_gather(hidden, "row", axis=0, tiled=True)
    member = (
        partition[:, None] == jnp.arange(part_gains.shape[0], dtype=jnp.int32)[None, :]
    ).astype(jnp.float32)
    row_gains = jnp.dot(member, part_gains, precision=lax.Precision.HIGHEST)
    upstream = cotangent.astype(jnp.float32) * row_gains
    partial_rows = slot_sum(*slots, panels, row_total, True)
    summed = lax.psum_scatter(
        partial_rows.astype(jnp.bfloat16), "col", scatter_dimension=0, tiled=True
    ).astype(jnp.float32)
    local_grad = (upstream * silu_slope(summed)).astype(jnp.bfloat16)
    agg_grad = lax.all_gather(local_grad, "col", axis=0, tiled=True)
    activated = jax.nn.silu(summed)
    layer_out = (activated * row_gains).astype(jnp.bfloat16)
    partial_cols = slot_sum(*slots, agg_grad, col_total, False)
    hidden_grad = lax.psum_scatter(
        partial_cols.astype(jnp.bfloat16), "row", scatter_dimension=0, tiled=True
    )
    feature_grad = lax.dot_general(
        hidden_grad, weight, (((1,), (1,)), ((), ())), preferred_element_type=jnp.float32
    ).astype(jnp.bfloat16)
    weight_part = lax.dot_general(
        features, hidden_grad, (((0,), (0,)), ((), ())), preferred_element_type=jnp.float32
    )
    part_terms = jnp.dot(
        member.T, cotangent.astype(jnp.float32) * activated, precision=lax.Precision.HIGHEST
    )
    part_sizes = jnp.sum(member, axis=0)
    weight_total, part_total, size_total = lax.psum(
        (weight_part, part_terms, part_sizes), ("row", "col")
    )
    total_nodes = node_count * lax.axis_size("row") * lax.axis_size("col")
    weight_grad = weight_total / jnp.sqrt(jnp.float32(total_nodes))
    gain_grad = part_total / jnp.sqrt(size_total)[:, None]
    return (layer_out, feature_grad, weight_grad, gain_grad)


def solution(mesh):
    row_count, col_count = mesh.shape["row"], mesh.shape["col"]

    def per_device(features, *others):
        share = features.shape[0]
        tile_bytes = 2 * share**2 * row_count * col_count
        sizes = (row_count, col_count, share // (BLOCK * CHUNKS))
        if tile_bytes <= 20 * MIB and all(n & (n - 1) == 0 < n for n in sizes):
            return dense_device(row_count, col_count, features, *others)
        return slot_device(features, *others)

    in_specs = (
        P(("row", "col"), None),
        P(),
        P("row", "col", None, None, None),
        P("row", "col", None),
        P("row", "col", None),
        P("row", "col"),
        P(),
        P(("row", "col")),
        P(("row", "col"), None),
    )
    out_specs = (P(("row", "col"), None), P(("row", "col"), None), P(), P())
    return jax.shard_map(
        per_device, mesh=mesh, in_specs=in_specs, out_specs=out_specs, check_vma=False
    )
```

```python
import functools
import math

import jax
import jax.numpy as jnp
from jax import lax
from jax.experimental import pallas as pl
from jax.experimental.pallas import tpu as pltpu
from jax.sharding import PartitionSpec as P

BLOCK = 128
GROUP = 16
HEAVY = 16
CHUNKS = 2
MIB = 1 << 20
LIGHT = pl.CostEstimate(flops=1, bytes_accessed=1, transcendentals=0)


def bits_of(count):
    return [1 << b for b in range(count.bit_length() - 1)]


def shift_of(count):
    return count.bit_length() - 1


def block_order(count):
    return list(range(1, count, 2)) + list(range(0, count, 2))


def build_kernel(layout, at_ref, live_ref, rows_ref, cols_ref, slots_ref, tile_ref, buf, total, counts, most, sems):
    owners, per_owner, per_chunk = layout
    live = live_ref[0, 0]
    groups = (live + GROUP - 1) // GROUP
    row_blocks, col_blocks = tile_ref.shape[0] // BLOCK, tile_ref.shape[1] // BLOCK

    def fetch(group):
        return pltpu.make_async_copy(
            slots_ref.at[0, 0, pl.ds(group * GROUP, GROUP)], buf.at[group], sems.at[group]
        )

    @pl.loop(0, groups)
    def _(group):
        fetch(group).start()

    zeros = jnp.zeros((BLOCK, tile_ref.shape[1]), tile_ref.dtype)
    most[0] = 0

    @pl.loop(0, row_blocks)
    def _(r):
        tile_ref[pl.ds(pl.multiple_of(r * BLOCK, BLOCK), BLOCK), :] = zeros
        for c in range(col_blocks):
            counts[r * col_blocks + c] = 0

    own_row, own_col = at_ref[0], at_ref[1]

    def place(index):
        row = rows_ref[0, 0, index]
        k, inner = (row >> shift_of(per_owner)) ^ own_col, row & (per_owner - 1)
        k = ((k & 1) ^ 1) * (owners // 2) + (k >> 1)
        chunk, inner = inner >> shift_of(per_chunk), inner & (per_chunk - 1)
        row = (((chunk << shift_of(owners)) + k) << shift_of(per_chunk)) + inner
        return row, cols_ref[0, 0, index] ^ (own_row << shift_of(per_owner))

    def block(row, col):
        top, left = pl.multiple_of(row * BLOCK, BLOCK), pl.multiple_of(col * BLOCK, BLOCK)
        return pl.ds(top, BLOCK), pl.ds(left, BLOCK)

    @pl.loop(0, groups)
    def _(group):
        fetch(group).wait()

        def add(s):
            row, col = place(group * GROUP + s)
            here = counts[row * col_blocks + col] + 1
            counts[row * col_blocks + col] = here
            tile_ref[block(row, col)] += buf[group, s]
            return here

        here = live - group * GROUP

        @pl.when(here >= GROUP)
        def _():
            most[0] = functools.reduce(jnp.maximum, [add(s) for s in range(GROUP)], most[0])

        @pl.when(here < GROUP)
        def _():
            @pl.loop(0, here)
            def _(s):
                most[0] = jnp.maximum(most[0], add(s))

    @pl.when(most[0] > HEAVY)
    def _():
        @pl.loop(0, live)
        def _(index):
            p_row, p_col = place(index)
            p = p_row * col_blocks + p_col

            @pl.when(counts[p] > HEAVY)
            def _():
                counts[p] = 0
                total[...] = jnp.zeros_like(total)

                @pl.loop(index, live)
                def _(other):
                    row, col = place(other)

                    @pl.when(row * col_blocks + col == p)
                    def _():
                        total[...] += buf[other >> shift_of(GROUP), other & (GROUP - 1)].astype(jnp.float32)

                tile_ref[block(p_row, p_col)] = total[...].astype(tile_ref.dtype)


def build_tile(at, slots, rows, cols, live, row_blocks, col_blocks, layout):
    smem = pl.BlockSpec(memory_space=pltpu.SMEM)
    vmem = pl.BlockSpec(memory_space=pltpu.VMEM)
    groups = slots.shape[2] // GROUP
    return pl.pallas_call(
        functools.partial(build_kernel, layout),
        out_shape=pltpu.VMEM((row_blocks * BLOCK, col_blocks * BLOCK), jnp.bfloat16),
        in_specs=[smem, smem, smem, smem, pl.BlockSpec(memory_space=pl.ANY)],
        out_specs=vmem,
        scratch_shapes=[
            pltpu.VMEM((groups, GROUP, BLOCK, BLOCK), jnp.bfloat16),
            pltpu.VMEM((BLOCK, BLOCK), jnp.float32),
            pltpu.SMEM((row_blocks * col_blocks,), jnp.int32),
            pltpu.SMEM((1,), jnp.int32),
            pltpu.SemaphoreType.DMA((groups,)),
        ],
        compiler_params=pltpu.CompilerParams(vmem_limit_bytes=36 * MIB),
        cost_estimate=pl.CostEstimate(flops=0, bytes_accessed=20 * MIB, transcendentals=0),
        name="build_tile",
    )(at, live, rows, cols, slots)


def forward_kernel(chunk, first, tile_ref, *refs):
    *feature_refs, panel = refs
    if first:
        before_ref, (*feature_refs, send_ref, rest_ref) = feature_refs[0], feature_refs[1:]
    else:
        *feature_refs, sum_ref = feature_refs
    share = feature_refs[0].shape[0]
    for r, feature_ref in enumerate(feature_refs):
        panel[r * share : (r + 1) * share, :] = feature_ref[...]
    rows = tile_ref.shape[0] // CHUNKS
    half = rows // 2
    for m in range(0, rows, half):
        block = tile_ref[chunk * rows + m : chunk * rows + m + half, first * share : first * share + panel.shape[0]]
        product = jnp.dot(block, panel[...], preferred_element_type=jnp.float32)
        if first:
            into = rest_ref if m else send_ref
            into[...] = (before_ref[m : m + half, :] + product).astype(jnp.bfloat16)
        else:
            sum_ref[m : m + half, :] = product


def forward(chunk, tile, features, first, before=None):
    share, width = features[0].shape
    rows = tile.shape[0] // CHUNKS
    vmem = pl.BlockSpec(memory_space=pltpu.VMEM)
    if first:
        given, out_shape = [before, *features], [pltpu.VMEM((rows // 2, width), jnp.bfloat16)] * 2
    else:
        given, out_shape = features, pltpu.VMEM((rows, width), jnp.float32)
    return pl.pallas_call(
        functools.partial(forward_kernel, chunk, first),
        out_shape=out_shape,
        in_specs=[vmem] * (1 + len(given)),
        out_specs=[vmem] * 2 if first else vmem,
        scratch_shapes=[pltpu.VMEM((len(features) * share, width), jnp.bfloat16)],
        compiler_params=pltpu.CompilerParams(vmem_limit_bytes=8 * MIB),
        cost_estimate=pl.CostEstimate(
            flops=2 * rows * len(features) * share * width, bytes_accessed=0, transcendentals=0
        ),
        name="forward",
    )(tile, *given)


def silu_slope(values):
    sig = jax.nn.sigmoid(values)
    return sig * (1.0 + values * (1.0 - sig))


def wide(values):
    return values.astype(jnp.float32)


def dot_last(left, right):
    return lax.dot_general(left, right, (((1,), (1,)), ((), ())), preferred_element_type=jnp.float32)


def combine_kernel(specs, *refs):
    out_refs = refs[-len(specs) :]
    for spec, out_ref in zip(specs, out_refs):
        total = None
        for source, start in spec:
            term = wide(refs[source][start : start + out_ref.shape[0], :])
            total = term if total is None else total + term
        out_ref[...] = total.astype(out_ref.dtype)


def combine(step, sums):
    sources = list({id(x): x for terms in sums for x, _ in terms}.values())
    at = {id(x): i for i, x in enumerate(sources)}
    specs = [[(at[id(x)], start) for x, start in terms] for terms in sums]
    vmem = pl.BlockSpec(memory_space=pltpu.VMEM)
    return pl.pallas_call(
        functools.partial(combine_kernel, specs),
        out_shape=[pltpu.VMEM((step, sources[0].shape[1]), jnp.bfloat16)] * len(sums),
        in_specs=[vmem] * len(sources),
        out_specs=[vmem] * len(sums),
        compiler_params=pltpu.CompilerParams(vmem_limit_bytes=4 * MIB),
        cost_estimate=LIGHT,
        name="combine",
    )(*sources)


def gate_kernel(chunk, starts, upstream_ref, weight_ref, *refs):
    *term_refs, turned_ref, grad_ref, rows_ref, summed_ref = refs
    step = grad_ref.shape[0]
    rows = None
    for term_ref, start in zip(term_refs, starts):
        term = wide(term_ref[start : start + step, :])
        rows = term if rows is None else rows + term
    high = rows.astype(jnp.bfloat16)
    low = (rows - wide(high)).astype(jnp.bfloat16)
    weight = weight_ref[...]
    summed = jnp.dot(high, weight, preferred_element_type=jnp.float32) + jnp.dot(
        low, weight, preferred_element_type=jnp.float32
    )
    upstream = upstream_ref[chunk * step : (chunk + 1) * step, :]
    grad = (upstream * silu_slope(summed)).astype(jnp.bfloat16)
    turned_ref[...] = dot_last(grad, weight).astype(jnp.bfloat16)
    grad_ref[...] = grad
    rows_ref[...] = high
    summed_ref[...] = summed


def gate(chunk, upstream, weight, terms):
    shape = (upstream.shape[0] // CHUNKS, upstream.shape[1])
    vmem = pl.BlockSpec(memory_space=pltpu.VMEM)
    return pl.pallas_call(
        functools.partial(gate_kernel, chunk, [start for _, start in terms]),
        out_shape=[pltpu.VMEM(shape, jnp.bfloat16)] * 3 + [pltpu.VMEM(shape, jnp.float32)],
        in_specs=[vmem] * (2 + len(terms)),
        out_specs=[vmem] * 4,
        compiler_params=pltpu.CompilerParams(vmem_limit_bytes=8 * MIB),
        cost_estimate=LIGHT,
        name="gate",
    )(upstream, weight, *(x for x, _ in terms))


def pack(values, exact_rows):
    exact = values[values.shape[0] - exact_rows :]
    high = exact.astype(jnp.bfloat16)
    low = (exact - wide(high)).astype(jnp.bfloat16)
    return jnp.concatenate([values[: -exact_rows].astype(jnp.bfloat16), high, low], axis=0)


def unpack(message, exact_rows):
    values = wide(message)
    rows = message.shape[0] - 2 * exact_rows
    exact = values[rows : rows + exact_rows] + values[rows + exact_rows :]
    return jnp.concatenate([values[:rows], exact], axis=0)


def local_sums(chunk, members_ref, cotangent_ref, rows_ref, grad_ref, summed_ref):
    step = rows_ref.shape[0]
    at = slice(chunk * step, (chunk + 1) * step)
    summed = summed_ref[...]
    activated = summed * jax.nn.sigmoid(summed)
    weight_part = lax.dot_general(
        rows_ref[...], grad_ref[...], (((0,), (0,)), ((), ())), preferred_element_type=jnp.float32
    )
    members = members_ref[:, at]
    part_terms = jnp.dot(
        members,
        wide(cotangent_ref[at, :]) * activated,
        precision=lax.Precision.HIGHEST,
        preferred_element_type=jnp.float32,
    )
    sizes = jnp.sum(members, axis=1, keepdims=True)
    return jnp.concatenate([weight_part, part_terms, jnp.broadcast_to(sizes, part_terms.shape)], axis=0)


def local_first_kernel(members_ref, cotangent_ref, *refs):
    *given, sums_ref = refs
    sums_ref[...] = local_sums(0, members_ref, cotangent_ref, *given)


def local_last_kernel(at_ref, members_ref, cotangent_ref, before_ref, *refs):
    *given, keep_ref, send_ref, sums = refs
    terms = local_sums(CHUNKS - 1, members_ref, cotangent_ref, *given)
    sums[...] = before_ref[...] + terms
    core = at_ref[1] & 1
    count = members_ref.shape[0]
    width = sums.shape[1]
    rows = width // 2
    for half, message_ref in ((core, keep_ref), (1 - core, send_ref)):
        top = sums[pl.ds(pl.multiple_of(half * rows, rows), rows), :]
        bottom = sums[pl.ds(pl.multiple_of(width + half * count, count), count), :]
        message_ref[...] = pack(jnp.concatenate([top, bottom], axis=0), count)


def local_terms(at, members, cotangent, chunks):
    width = cotangent.shape[1]
    count = members.shape[0]
    vmem = pl.BlockSpec(memory_space=pltpu.VMEM)
    smem = pl.BlockSpec(memory_space=pltpu.SMEM)
    first, last = chunks
    sums = jax.ShapeDtypeStruct((width + 2 * count, width), jnp.float32)
    before = pl.pallas_call(
        local_first_kernel,
        out_shape=pltpu.VMEM(sums.shape, sums.dtype),
        in_specs=[vmem] * 5,
        out_specs=vmem,
        compiler_params=pltpu.CompilerParams(vmem_limit_bytes=8 * MIB),
        cost_estimate=LIGHT,
        name="local_first",
    )(members, cotangent, *first)
    message = pltpu.VMEM((width // 2 + 2 * count, width), jnp.bfloat16)
    return pl.pallas_call(
        local_last_kernel,
        out_shape=[message, message],
        in_specs=[smem] + [vmem] * 6,
        out_specs=[vmem] * 2,
        scratch_shapes=[pltpu.VMEM(sums.shape, sums.dtype)],
        compiler_params=pltpu.CompilerParams(vmem_limit_bytes=8 * MIB),
        cost_estimate=LIGHT,
        name="local_last",
    )(at, members, cotangent, before, *last)


def output_kernel(gains_ref, *refs):
    *summed_refs, out_ref = refs
    step = summed_refs[0].shape[0]
    for n, summed_ref in enumerate(summed_refs):
        at = slice(n * step, (n + 1) * step)
        summed = summed_ref[...]
        out_ref[at, :] = (summed * jax.nn.sigmoid(summed) * gains_ref[at, :]).astype(out_ref.dtype)


def output(gains, summed):
    vmem = pl.BlockSpec(memory_space=pltpu.VMEM)
    return pl.pallas_call(
        output_kernel,
        out_shape=jax.ShapeDtypeStruct(gains.shape, jnp.bfloat16),
        in_specs=[vmem] * (1 + len(summed)),
        out_specs=vmem,
        compiler_params=pltpu.CompilerParams(vmem_limit_bytes=8 * MIB),
        cost_estimate=LIGHT,
        name="output",
    )(gains, *summed)


def add_kernel(exact_rows, own_ref, other_ref, out_ref):
    out_ref[...] = pack(
        unpack(own_ref[...], exact_rows) + unpack(other_ref[...], exact_rows), exact_rows
    )


def add_messages(exact_rows, own, other):
    vmem = pl.BlockSpec(memory_space=pltpu.VMEM)
    return pl.pallas_call(
        functools.partial(add_kernel, exact_rows),
        out_shape=pltpu.VMEM(own.shape, jnp.bfloat16),
        in_specs=[vmem] * 2,
        out_specs=vmem,
        compiler_params=pltpu.CompilerParams(vmem_limit_bytes=4 * MIB),
        cost_estimate=LIGHT,
        name="add_messages",
    )(own, other)


def totals_kernel(exact_rows, scale, at_ref, own_ref, other_ref, weight_ref, gain_ref, exact):
    core = at_ref[1] & 1
    rows = weight_ref.shape[0] // 2
    for half, message_ref in ((core, own_ref), (1 - core, other_ref)):
        values = unpack(message_ref[...], exact_rows)
        weight_ref[pl.ds(pl.multiple_of(half * rows, rows), rows), :] = values[:rows] * scale
        exact[pl.ds(pl.multiple_of(half * exact_rows, exact_rows), exact_rows), :] = values[rows:]
    gain_ref[...] = exact[:exact_rows, :] / jnp.sqrt(exact[exact_rows:, :])


def totals(exact_rows, scale, at, own, other):
    width = own.shape[1]
    vmem = pl.BlockSpec(memory_space=pltpu.VMEM)
    smem = pl.BlockSpec(memory_space=pltpu.SMEM)
    return pl.pallas_call(
        functools.partial(totals_kernel, exact_rows, scale),
        out_shape=[
            jax.ShapeDtypeStruct((width, width), jnp.float32),
            jax.ShapeDtypeStruct((exact_rows, width), jnp.float32),
        ],
        in_specs=[smem] + [vmem] * 2,
        out_specs=[vmem] * 2,
        scratch_shapes=[pltpu.VMEM((2 * exact_rows, width), jnp.float32)],
        compiler_params=pltpu.CompilerParams(vmem_limit_bytes=4 * MIB),
        cost_estimate=LIGHT,
        name="totals",
    )(at, own, other)


def backward_kernel(chunk, targets, places, tile_ref, *refs):
    given, out_refs = refs[: -len(targets) - 1], refs[-len(targets) - 1 :]
    before_refs, block_refs = given[: len(given) - len(places)], given[len(given) - len(places) :]
    *part_refs, panel = out_refs
    for block_ref, (source, target, rows) in zip(block_refs, places):
        panel[target : target + rows, :] = block_ref[source : source + rows, :]
    share = part_refs[0].shape[0]
    depth = panel.shape[0]
    for i, r in enumerate(targets):
        product = lax.dot_general(
            tile_ref[chunk * depth : (chunk + 1) * depth, r * share : (r + 1) * share],
            panel[...],
            (((0,), (0,)), ((), ())),
            preferred_element_type=jnp.float32,
        )
        if before_refs:
            product = product + before_refs[i][...]
        part_refs[i][...] = product.astype(part_refs[i].dtype)


def backward(chunk, targets, kinds, tile, blocks, places, before, share):
    width = blocks[0].shape[1]
    depth = tile.shape[0] // CHUNKS
    vmem = pl.BlockSpec(memory_space=pltpu.VMEM)
    flops = (1 if chunk else 2) * depth * len(targets) * share * width
    return pl.pallas_call(
        functools.partial(backward_kernel, chunk, targets, places),
        out_shape=[pltpu.VMEM((share, width), kind) for kind in kinds]
        + [pltpu.VMEM((depth, width), jnp.bfloat16)],
        in_specs=[vmem] * (1 + len(before) + len(blocks)),
        out_specs=[vmem] * (len(targets) + 1),
        compiler_params=pltpu.CompilerParams(vmem_limit_bytes=8 * MIB),
        cost_estimate=pl.CostEstimate(flops=flops, bytes_accessed=0, transcendentals=0),
        name="backward",
    )(tile, *before, *blocks)


def finish_kernel(*refs):
    *part_refs, out_ref = refs
    total = None
    for part_ref in part_refs:
        term = wide(part_ref[...])
        total = term if total is None else total + term
    out_ref[...] = total.astype(out_ref.dtype)


def finish(parts):
    vmem = pl.BlockSpec(memory_space=pltpu.VMEM)
    return pl.pallas_call(
        finish_kernel,
        out_shape=jax.ShapeDtypeStruct(parts[0].shape, jnp.bfloat16),
        in_specs=[vmem] * len(parts),
        out_specs=vmem,
        compiler_params=pltpu.CompilerParams(vmem_limit_bytes=8 * MIB),
        cost_estimate=LIGHT,
        name="finish",
    )(*parts)


def swap(values, axis, mask, count):
    return lax.ppermute(values, axis, [(d, d ^ mask) for d in range(count)])


def after(values, *others):
    return lax.optimization_barrier((values, *others))[0]


def dense_device(
    row_count,
    col_count,
    features,
    weight,
    adjacency,
    block_rows,
    block_cols,
    live_blocks,
    part_gains,
    partition,
    cotangent,
):
    share, width = features.shape
    step = share // CHUNKS
    row_blocks = share * col_count // BLOCK
    at = jnp.stack([lax.axis_index("row"), lax.axis_index("col")]).astype(jnp.int32)
    gathered = [features] + [swap(features, "row", r, row_count) for r in range(1, row_count)]
    layout = (col_count, share // BLOCK, step // BLOCK)
    tile = build_tile(
        at, adjacency, block_rows, block_cols, live_blocks, row_blocks, share * row_count // BLOCK, layout
    )
    part_count = part_gains.shape[0]
    members = (
        partition[None, :] == jnp.arange(part_count, dtype=jnp.int32)[:, None]
    ).astype(jnp.float32)
    row_gains = lax.dot_general(
        members, part_gains, (((0,), (0,)), ((), ())), precision=lax.Precision.HIGHEST
    )
    upstream = wide(cotangent) * row_gains

    order = block_order(col_count)
    col_bits = bits_of(col_count)
    chunks = range(CHUNKS)
    early = row_count // 2
    sums = [forward(n, tile, gathered[:early], 0) for n in chunks]
    pending = []
    for n in chunks:
        send, rest = forward(n, tile, gathered[early:], early, sums[n])
        other = swap(send, "col", col_bits[0], col_count)
        kept = enumerate(order[len(order) // 2 :])
        pending.append({k: [(rest, t * step), (other, t * step)] for t, k in kept})
    last = None
    for bit in col_bits[1:]:
        for terms in pending:
            blocks = sorted((k for k in terms if k & bit), reverse=True)
            sums = [terms.pop(k) for k in blocks]
            if last is not None:
                x, start = sums[0][-1]
                sums[0][-1] = (after(x, last), start)
            outs = combine(step, sums)
            last = outs[0]
            for k, out in zip(blocks, outs):
                terms[k ^ bit].append((swap(out, "col", bit, col_count), 0))
    gated, held = [], []
    for n in chunks:
        gated.append(gate(n, after(upstream, last), weight, pending[n][0]))
        last = gated[-1][0]
        held.append({0: last})
    scale = 1.0 / math.sqrt(share * row_count * col_count)
    local = [(rows, grad, summed) for _, grad, rows, summed in gated]
    message, out = local_terms(at, members, cotangent, local)
    other = swap(out, "col", col_bits[0], col_count)
    messages = [add_messages(part_count, message, other)]
    for bit in reversed(col_bits[1:]):
        for n in chunks:
            for k in list(held[n]):
                sent = held[n][k]
                if k and n == 0:
                    sent = after(sent, message)
                if k and n:
                    sent = after(sent, messages[0], *held[n].values())
                held[n][k ^ bit] = swap(sent, "col", bit, col_count)
    stages = [("row", bit, row_count) for bit in bits_of(row_count)]
    stages += [("col", bit, col_count) for bit in col_bits[1:]]
    for stage in stages:
        messages.append(add_messages(part_count, messages[-1], swap(messages[-1], *stage)))
    other = swap(messages[-1], "col", col_bits[0], col_count)
    weight_grad, gain_grad = totals(part_count, scale, at, messages[-1], other)

    layer_out = output(after(row_gains, messages[4]), [g[3] for g in gated])
    sums = []
    bit = col_bits[0]
    for n in chunks:
        blocks, places = [], []
        *ready, late = held[n]
        for group in (ready, [late]):
            sent = jnp.concatenate([held[n][k] for k in group], axis=0)
            if n and group is not ready:
                sent = after(sent, messages[2])
            arrived = swap(sent, "col", bit, col_count)
            for t, k in enumerate(group):
                blocks += [held[n][k], arrived]
                places += [(0, order.index(k) * step, step), (t * step, order.index(k ^ bit) * step, step)]
        rows = list(range(row_count))
        if n < CHUNKS - 1:
            kinds = [jnp.float32] * row_count
            *sums, _ = backward(n, rows, kinds, tile, blocks, places, sums, share)
    parts = [None] * row_count
    farthest = row_count - 1
    for targets in ([farthest], rows[1:farthest], [0]):
        if not targets:
            continue
        kinds = [jnp.float32 if r == 0 else jnp.bfloat16 for r in targets]
        *outs, panel = backward(
            CHUNKS - 1, targets, kinds, tile, blocks, places, [sums[r] for r in targets], share
        )
        blocks, places = [after(panel, messages[3], *outs)], [(0, 0, panel.shape[0])]
        for r, out in zip(targets, outs):
            parts[r] = swap(out, "row", r, row_count) if r else out
    feature_grad = finish(parts)

    return (layer_out, feature_grad, weight_grad, gain_grad)


def slot_sum(tile_values, row_index, col_index, live_count, panels, out_blocks, forward_way):
    slot_count = tile_values.shape[0]
    feature_width = panels.shape[1]
    panel_blocks = panels.reshape(-1, BLOCK, feature_width)

    def one_slot(slot, totals):
        values = lax.dynamic_index_in_dim(tile_values, slot, 0, keepdims=False)
        source, target = col_index[slot], row_index[slot]
        if not forward_way:
            values, source, target = values.T, target, source
        panel = lax.dynamic_index_in_dim(panel_blocks, source, 0, keepdims=False)
        product = jnp.dot(values, panel, preferred_element_type=jnp.float32)
        return totals.at[target].add(product)

    start = jnp.zeros((out_blocks, BLOCK, feature_width), jnp.float32)
    totals = lax.fori_loop(0, jnp.minimum(live_count, slot_count), one_slot, start)
    return totals.reshape(out_blocks * BLOCK, feature_width)


def slot_device(
    features,
    weight,
    adjacency,
    block_rows,
    block_cols,
    live_blocks,
    part_gains,
    partition,
    cotangent,
):
    node_count = features.shape[0]
    row_total = node_count * lax.axis_size("col") // BLOCK
    col_total = node_count * lax.axis_size("row") // BLOCK
    slots = (adjacency[0, 0], block_rows[0, 0], block_cols[0, 0], live_blocks[0, 0])
    hidden = jnp.dot(features, weight, preferred_element_type=jnp.float32).astype(jnp.bfloat16)
    panels = lax.all_gather(hidden, "row", axis=0, tiled=True)
    member = (
        partition[:, None] == jnp.arange(part_gains.shape[0], dtype=jnp.int32)[None, :]
    ).astype(jnp.float32)
    row_gains = jnp.dot(member, part_gains, precision=lax.Precision.HIGHEST)
    upstream = cotangent.astype(jnp.float32) * row_gains
    partial_rows = slot_sum(*slots, panels, row_total, True)
    summed = lax.psum_scatter(
        partial_rows.astype(jnp.bfloat16), "col", scatter_dimension=0, tiled=True
    ).astype(jnp.float32)
    local_grad = (upstream * silu_slope(summed)).astype(jnp.bfloat16)
    agg_grad = lax.all_gather(local_grad, "col", axis=0, tiled=True)
    activated = jax.nn.silu(summed)
    layer_out = (activated * row_gains).astype(jnp.bfloat16)
    partial_cols = slot_sum(*slots, agg_grad, col_total, False)
    hidden_grad = lax.psum_scatter(
        partial_cols.astype(jnp.bfloat16), "row", scatter_dimension=0, tiled=True
    )
    feature_grad = lax.dot_general(
        hidden_grad, weight, (((1,), (1,)), ((), ())), preferred_element_type=jnp.float32
    ).astype(jnp.bfloat16)
    weight_part = lax.dot_general(
        features, hidden_grad, (((0,), (0,)), ((), ())), preferred_element_type=jnp.float32
    )
    part_terms = jnp.dot(
        member.T, cotangent.astype(jnp.float32) * activated, precision=lax.Precision.HIGHEST
    )
    part_sizes = jnp.sum(member, axis=0)
    weight_total, part_total, size_total = lax.psum(
        (weight_part, part_terms, part_sizes), ("row", "col")
    )
    total_nodes = node_count * lax.axis_size("row") * lax.axis_size("col")
    weight_grad = weight_total / jnp.sqrt(jnp.float32(total_nodes))
    gain_grad = part_total / jnp.sqrt(size_total)[:, None]
    return (layer_out, feature_grad, weight_grad, gain_grad)


def solution(mesh):
    row_count, col_count = mesh.shape["row"], mesh.shape["col"]

    def per_device(features, *others):
        share = features.shape[0]
        tile_bytes = 2 * share**2 * row_count * col_count
        sizes = (row_count // 2, col_count // 2, share // (BLOCK * CHUNKS))
        whole = share % (BLOCK * CHUNKS) == 0 and others[1].shape[2] % GROUP == 0
        if tile_bytes <= 20 * MIB and whole and all(n & (n - 1) == 0 < n for n in sizes):
            return dense_device(row_count, col_count, features, *others)
        return slot_device(features, *others)

    in_specs = (
        P(("row", "col"), None),
        P(),
        P("row", "col", None, None, None),
        P("row", "col", None),
        P("row", "col", None),
        P("row", "col"),
        P(),
        P(("row", "col")),
        P(("row", "col"), None),
    )
    out_specs = (P(("row", "col"), None), P(("row", "col"), None), P(), P())
    return jax.shard_map(
        per_device, mesh=mesh, in_specs=in_specs, out_specs=out_specs, check_vma=False
    )
```

```python
import functools
import math

import jax
import jax.numpy as jnp
from jax import lax
from jax.experimental import pallas as pl
from jax.experimental.pallas import tpu as pltpu
from jax.sharding import PartitionSpec as P

BLOCK = 128
GROUP = 16
HEAVY = 16
CHUNKS = 2
MIB = 1 << 20
LIGHT = pl.CostEstimate(flops=1, bytes_accessed=1, transcendentals=0)


def bits_of(count):
    return [1 << b for b in range(count.bit_length() - 1)]


def shift_of(count):
    return count.bit_length() - 1


def block_order(count):
    return list(range(1, count, 2)) + list(range(0, count, 2))


def build_kernel(layout, at_ref, live_ref, rows_ref, cols_ref, slots_ref, tile_ref, buf, total, counts, most, sems):
    owners, per_owner, per_chunk = layout
    live = live_ref[0, 0]
    groups = (live + GROUP - 1) // GROUP
    row_blocks, col_blocks = tile_ref.shape[0] // BLOCK, tile_ref.shape[1] // BLOCK

    def fetch(group):
        return pltpu.make_async_copy(
            slots_ref.at[0, 0, pl.ds(group * GROUP, GROUP)], buf.at[group], sems.at[group]
        )

    @pl.loop(0, groups)
    def _(group):
        fetch(group).start()

    zeros = jnp.zeros((BLOCK, tile_ref.shape[1]), tile_ref.dtype)
    most[0] = 0

    @pl.loop(0, row_blocks)
    def _(r):
        tile_ref[pl.ds(pl.multiple_of(r * BLOCK, BLOCK), BLOCK), :] = zeros
        for c in range(col_blocks):
            counts[r * col_blocks + c] = 0

    own_row, own_col = at_ref[0], at_ref[1]

    def place(index):
        row = rows_ref[0, 0, index]
        k, inner = (row >> shift_of(per_owner)) ^ own_col, row & (per_owner - 1)
        k = ((k & 1) ^ 1) * (owners // 2) + (k >> 1)
        chunk, inner = inner >> shift_of(per_chunk), inner & (per_chunk - 1)
        row = (((chunk << shift_of(owners)) + k) << shift_of(per_chunk)) + inner
        return row, cols_ref[0, 0, index] ^ (own_row << shift_of(per_owner))

    def block(row, col):
        top, left = pl.multiple_of(row * BLOCK, BLOCK), pl.multiple_of(col * BLOCK, BLOCK)
        return pl.ds(top, BLOCK), pl.ds(left, BLOCK)

    @pl.loop(0, groups)
    def _(group):
        fetch(group).wait()

        def add(s):
            row, col = place(group * GROUP + s)
            here = counts[row * col_blocks + col] + 1
            counts[row * col_blocks + col] = here
            tile_ref[block(row, col)] += buf[group, s]
            return here

        here = live - group * GROUP

        @pl.when(here >= GROUP)
        def _():
            most[0] = functools.reduce(jnp.maximum, [add(s) for s in range(GROUP)], most[0])

        @pl.when(here < GROUP)
        def _():
            @pl.loop(0, here)
            def _(s):
                most[0] = jnp.maximum(most[0], add(s))

    @pl.when(most[0] > HEAVY)
    def _():
        @pl.loop(0, live)
        def _(index):
            p_row, p_col = place(index)
            p = p_row * col_blocks + p_col

            @pl.when(counts[p] > HEAVY)
            def _():
                counts[p] = 0
                total[...] = jnp.zeros_like(total)

                @pl.loop(index, live)
                def _(other):
                    row, col = place(other)

                    @pl.when(row * col_blocks + col == p)
                    def _():
                        total[...] += buf[other >> shift_of(GROUP), other & (GROUP - 1)].astype(jnp.float32)

                tile_ref[block(p_row, p_col)] = total[...].astype(tile_ref.dtype)


def build_tile(at, slots, rows, cols, live, row_blocks, col_blocks, layout):
    smem = pl.BlockSpec(memory_space=pltpu.SMEM)
    vmem = pl.BlockSpec(memory_space=pltpu.VMEM)
    groups = slots.shape[2] // GROUP
    return pl.pallas_call(
        functools.partial(build_kernel, layout),
        out_shape=pltpu.VMEM((row_blocks * BLOCK, col_blocks * BLOCK), jnp.bfloat16),
        in_specs=[smem, smem, smem, smem, pl.BlockSpec(memory_space=pl.ANY)],
        out_specs=vmem,
        scratch_shapes=[
            pltpu.VMEM((groups, GROUP, BLOCK, BLOCK), jnp.bfloat16),
            pltpu.VMEM((BLOCK, BLOCK), jnp.float32),
            pltpu.SMEM((row_blocks * col_blocks,), jnp.int32),
            pltpu.SMEM((1,), jnp.int32),
            pltpu.SemaphoreType.DMA((groups,)),
        ],
        compiler_params=pltpu.CompilerParams(vmem_limit_bytes=36 * MIB),
        cost_estimate=pl.CostEstimate(flops=0, bytes_accessed=20 * MIB, transcendentals=0),
        name="build_tile",
    )(at, live, rows, cols, slots)


def forward_kernel(chunk, first, tile_ref, *refs):
    *feature_refs, panel = refs
    if first:
        before_ref, (*feature_refs, send_ref, rest_ref) = feature_refs[0], feature_refs[1:]
    else:
        *feature_refs, sum_ref = feature_refs
    share = feature_refs[0].shape[0]
    for r, feature_ref in enumerate(feature_refs):
        panel[r * share : (r + 1) * share, :] = feature_ref[...]
    rows = tile_ref.shape[0] // CHUNKS
    half = rows // 2
    for m in range(0, rows, half):
        block = tile_ref[chunk * rows + m : chunk * rows + m + half, first * share : first * share + panel.shape[0]]
        product = jnp.dot(block, panel[...], preferred_element_type=jnp.float32)
        if first:
            into = rest_ref if m else send_ref
            into[...] = (before_ref[m : m + half, :] + product).astype(jnp.bfloat16)
        else:
            sum_ref[m : m + half, :] = product


def forward(chunk, tile, features, first, before=None):
    share, width = features[0].shape
    rows = tile.shape[0] // CHUNKS
    vmem = pl.BlockSpec(memory_space=pltpu.VMEM)
    if first:
        given, out_shape = [before, *features], [pltpu.VMEM((rows // 2, width), jnp.bfloat16)] * 2
    else:
        given, out_shape = features, pltpu.VMEM((rows, width), jnp.float32)
    return pl.pallas_call(
        functools.partial(forward_kernel, chunk, first),
        out_shape=out_shape,
        in_specs=[vmem] * (1 + len(given)),
        out_specs=[vmem] * 2 if first else vmem,
        scratch_shapes=[pltpu.VMEM((len(features) * share, width), jnp.bfloat16)],
        compiler_params=pltpu.CompilerParams(vmem_limit_bytes=8 * MIB),
        cost_estimate=pl.CostEstimate(
            flops=2 * rows * len(features) * share * width, bytes_accessed=0, transcendentals=0
        ),
        name="forward",
    )(tile, *given)


def silu_slope(values):
    sig = jax.nn.sigmoid(values)
    return sig * (1.0 + values * (1.0 - sig))


def wide(values):
    return values.astype(jnp.float32)


def dot_last(left, right):
    return lax.dot_general(left, right, (((1,), (1,)), ((), ())), preferred_element_type=jnp.float32)


def combine_kernel(specs, *refs):
    out_refs = refs[-len(specs) :]
    for spec, out_ref in zip(specs, out_refs):
        total = None
        for source, start in spec:
            term = wide(refs[source][start : start + out_ref.shape[0], :])
            total = term if total is None else total + term
        out_ref[...] = total.astype(out_ref.dtype)


def combine(step, sums):
    sources = list({id(x): x for terms in sums for x, _ in terms}.values())
    at = {id(x): i for i, x in enumerate(sources)}
    specs = [[(at[id(x)], start) for x, start in terms] for terms in sums]
    vmem = pl.BlockSpec(memory_space=pltpu.VMEM)
    return pl.pallas_call(
        functools.partial(combine_kernel, specs),
        out_shape=[pltpu.VMEM((step, sources[0].shape[1]), jnp.bfloat16)] * len(sums),
        in_specs=[vmem] * len(sources),
        out_specs=[vmem] * len(sums),
        compiler_params=pltpu.CompilerParams(vmem_limit_bytes=4 * MIB),
        cost_estimate=LIGHT,
        name="combine",
    )(*sources)


def gate_kernel(chunk, starts, upstream_ref, weight_ref, *refs):
    *term_refs, turned_ref, grad_ref, rows_ref, summed_ref = refs
    step = grad_ref.shape[0]
    rows = None
    for term_ref, start in zip(term_refs, starts):
        term = wide(term_ref[start : start + step, :])
        rows = term if rows is None else rows + term
    high = rows.astype(jnp.bfloat16)
    low = (rows - wide(high)).astype(jnp.bfloat16)
    weight = weight_ref[...]
    summed = jnp.dot(high, weight, preferred_element_type=jnp.float32) + jnp.dot(
        low, weight, preferred_element_type=jnp.float32
    )
    upstream = upstream_ref[chunk * step : (chunk + 1) * step, :]
    grad = (upstream * silu_slope(summed)).astype(jnp.bfloat16)
    turned_ref[...] = dot_last(grad, weight).astype(jnp.bfloat16)
    grad_ref[...] = grad
    rows_ref[...] = high
    summed_ref[...] = summed


def gate(chunk, upstream, weight, terms):
    shape = (upstream.shape[0] // CHUNKS, upstream.shape[1])
    vmem = pl.BlockSpec(memory_space=pltpu.VMEM)
    return pl.pallas_call(
        functools.partial(gate_kernel, chunk, [start for _, start in terms]),
        out_shape=[pltpu.VMEM(shape, jnp.bfloat16)] * 3 + [pltpu.VMEM(shape, jnp.float32)],
        in_specs=[vmem] * (2 + len(terms)),
        out_specs=[vmem] * 4,
        compiler_params=pltpu.CompilerParams(vmem_limit_bytes=8 * MIB),
        cost_estimate=LIGHT,
        name="gate",
    )(upstream, weight, *(x for x, _ in terms))


def pack(values, exact_rows):
    exact = values[values.shape[0] - exact_rows :]
    high = exact.astype(jnp.bfloat16)
    low = (exact - wide(high)).astype(jnp.bfloat16)
    return jnp.concatenate([values[: -exact_rows].astype(jnp.bfloat16), high, low], axis=0)


def unpack(message, exact_rows):
    values = wide(message)
    rows = message.shape[0] - 2 * exact_rows
    exact = values[rows : rows + exact_rows] + values[rows + exact_rows :]
    return jnp.concatenate([values[:rows], exact], axis=0)


def local_sums(chunk, members_ref, cotangent_ref, rows_ref, grad_ref, summed_ref):
    step = rows_ref.shape[0]
    at = slice(chunk * step, (chunk + 1) * step)
    summed = summed_ref[...]
    activated = summed * jax.nn.sigmoid(summed)
    weight_part = lax.dot_general(
        rows_ref[...], grad_ref[...], (((0,), (0,)), ((), ())), preferred_element_type=jnp.float32
    )
    members = members_ref[:, at]
    part_terms = jnp.dot(
        members,
        wide(cotangent_ref[at, :]) * activated,
        precision=lax.Precision.HIGHEST,
        preferred_element_type=jnp.float32,
    )
    sizes = jnp.sum(members, axis=1, keepdims=True)
    return jnp.concatenate([weight_part, part_terms, jnp.broadcast_to(sizes, part_terms.shape)], axis=0)


def local_first_kernel(members_ref, cotangent_ref, *refs):
    *given, sums_ref = refs
    sums_ref[...] = local_sums(0, members_ref, cotangent_ref, *given)


def local_last_kernel(at_ref, members_ref, cotangent_ref, before_ref, *refs):
    *given, keep_ref, send_ref, sums = refs
    terms = local_sums(CHUNKS - 1, members_ref, cotangent_ref, *given)
    sums[...] = before_ref[...] + terms
    core = at_ref[1] & 1
    count = members_ref.shape[0]
    width = sums.shape[1]
    rows = width // 2
    for half, message_ref in ((core, keep_ref), (1 - core, send_ref)):
        top = sums[pl.ds(pl.multiple_of(half * rows, rows), rows), :]
        bottom = sums[pl.ds(pl.multiple_of(width + half * count, count), count), :]
        message_ref[...] = pack(jnp.concatenate([top, bottom], axis=0), count)


def local_terms(at, members, cotangent, chunks):
    width = cotangent.shape[1]
    count = members.shape[0]
    vmem = pl.BlockSpec(memory_space=pltpu.VMEM)
    smem = pl.BlockSpec(memory_space=pltpu.SMEM)
    first, last = chunks
    sums = jax.ShapeDtypeStruct((width + 2 * count, width), jnp.float32)
    before = pl.pallas_call(
        local_first_kernel,
        out_shape=pltpu.VMEM(sums.shape, sums.dtype),
        in_specs=[vmem] * 5,
        out_specs=vmem,
        compiler_params=pltpu.CompilerParams(vmem_limit_bytes=8 * MIB),
        cost_estimate=LIGHT,
        name="local_first",
    )(members, cotangent, *first)
    message = pltpu.VMEM((width // 2 + 2 * count, width), jnp.bfloat16)
    return pl.pallas_call(
        local_last_kernel,
        out_shape=[message, message],
        in_specs=[smem] + [vmem] * 6,
        out_specs=[vmem] * 2,
        scratch_shapes=[pltpu.VMEM(sums.shape, sums.dtype)],
        compiler_params=pltpu.CompilerParams(vmem_limit_bytes=8 * MIB),
        cost_estimate=LIGHT,
        name="local_last",
    )(at, members, cotangent, before, *last)


def output_kernel(gains_ref, *refs):
    *summed_refs, out_ref = refs
    step = summed_refs[0].shape[0]
    for n, summed_ref in enumerate(summed_refs):
        at = slice(n * step, (n + 1) * step)
        summed = summed_ref[...]
        out_ref[at, :] = (summed * jax.nn.sigmoid(summed) * gains_ref[at, :]).astype(out_ref.dtype)


def output(gains, summed):
    vmem = pl.BlockSpec(memory_space=pltpu.VMEM)
    return pl.pallas_call(
        output_kernel,
        out_shape=jax.ShapeDtypeStruct(gains.shape, jnp.bfloat16),
        in_specs=[vmem] * (1 + len(summed)),
        out_specs=vmem,
        compiler_params=pltpu.CompilerParams(vmem_limit_bytes=8 * MIB),
        cost_estimate=LIGHT,
        name="output",
    )(gains, *summed)


def add_kernel(exact_rows, own_ref, other_ref, out_ref):
    out_ref[...] = pack(
        unpack(own_ref[...], exact_rows) + unpack(other_ref[...], exact_rows), exact_rows
    )


def add_messages(exact_rows, own, other):
    vmem = pl.BlockSpec(memory_space=pltpu.VMEM)
    return pl.pallas_call(
        functools.partial(add_kernel, exact_rows),
        out_shape=pltpu.VMEM(own.shape, jnp.bfloat16),
        in_specs=[vmem] * 2,
        out_specs=vmem,
        compiler_params=pltpu.CompilerParams(vmem_limit_bytes=4 * MIB),
        cost_estimate=LIGHT,
        name="add_messages",
    )(own, other)


def totals_kernel(exact_rows, scale, at_ref, own_ref, other_ref, weight_ref, gain_ref, exact):
    core = at_ref[1] & 1
    rows = weight_ref.shape[0] // 2
    for half, message_ref in ((core, own_ref), (1 - core, other_ref)):
        values = unpack(message_ref[...], exact_rows)
        weight_ref[pl.ds(pl.multiple_of(half * rows, rows), rows), :] = values[:rows] * scale
        exact[pl.ds(pl.multiple_of(half * exact_rows, exact_rows), exact_rows), :] = values[rows:]
    gain_ref[...] = exact[:exact_rows, :] / jnp.sqrt(exact[exact_rows:, :])


def totals(exact_rows, scale, at, own, other):
    width = own.shape[1]
    vmem = pl.BlockSpec(memory_space=pltpu.VMEM)
    smem = pl.BlockSpec(memory_space=pltpu.SMEM)
    return pl.pallas_call(
        functools.partial(totals_kernel, exact_rows, scale),
        out_shape=[
            jax.ShapeDtypeStruct((width, width), jnp.float32),
            jax.ShapeDtypeStruct((exact_rows, width), jnp.float32),
        ],
        in_specs=[smem] + [vmem] * 2,
        out_specs=[vmem] * 2,
        scratch_shapes=[pltpu.VMEM((2 * exact_rows, width), jnp.float32)],
        compiler_params=pltpu.CompilerParams(vmem_limit_bytes=4 * MIB),
        cost_estimate=LIGHT,
        name="totals",
    )(at, own, other)


def backward_kernel(chunk, targets, places, tile_ref, *refs):
    given, out_refs = refs[: -len(targets) - 1], refs[-len(targets) - 1 :]
    before_refs, block_refs = given[: len(given) - len(places)], given[len(given) - len(places) :]
    *part_refs, panel = out_refs
    for block_ref, (source, target, rows) in zip(block_refs, places):
        panel[target : target + rows, :] = block_ref[source : source + rows, :]
    share = part_refs[0].shape[0]
    depth = panel.shape[0]
    for i, r in enumerate(targets):
        product = lax.dot_general(
            tile_ref[chunk * depth : (chunk + 1) * depth, r * share : (r + 1) * share],
            panel[...],
            (((0,), (0,)), ((), ())),
            preferred_element_type=jnp.float32,
        )
        if before_refs:
            product = product + before_refs[i][...]
        part_refs[i][...] = product.astype(part_refs[i].dtype)


def backward(chunk, targets, kinds, tile, blocks, places, before, share):
    width = blocks[0].shape[1]
    depth = tile.shape[0] // CHUNKS
    vmem = pl.BlockSpec(memory_space=pltpu.VMEM)
    scale = 2 if chunk == 0 else 8 if len(targets) > 1 else 1
    flops = scale * depth * len(targets) * share * width
    return pl.pallas_call(
        functools.partial(backward_kernel, chunk, targets, places),
        out_shape=[pltpu.VMEM((share, width), kind) for kind in kinds]
        + [pltpu.VMEM((depth, width), jnp.bfloat16)],
        in_specs=[vmem] * (1 + len(before) + len(blocks)),
        out_specs=[vmem] * (len(targets) + 1),
        compiler_params=pltpu.CompilerParams(vmem_limit_bytes=8 * MIB),
        cost_estimate=pl.CostEstimate(flops=flops, bytes_accessed=0, transcendentals=0),
        name="backward",
    )(tile, *before, *blocks)


def finish_kernel(*refs):
    *part_refs, out_ref = refs
    total = None
    for part_ref in part_refs:
        term = wide(part_ref[...])
        total = term if total is None else total + term
    out_ref[...] = total.astype(out_ref.dtype)


def finish(parts):
    vmem = pl.BlockSpec(memory_space=pltpu.VMEM)
    return pl.pallas_call(
        finish_kernel,
        out_shape=jax.ShapeDtypeStruct(parts[0].shape, jnp.bfloat16),
        in_specs=[vmem] * len(parts),
        out_specs=vmem,
        compiler_params=pltpu.CompilerParams(vmem_limit_bytes=8 * MIB),
        cost_estimate=LIGHT,
        name="finish",
    )(*parts)


def swap(values, axis, mask, count):
    return lax.ppermute(values, axis, [(d, d ^ mask) for d in range(count)])


def after(values, *others):
    return lax.optimization_barrier((values, *others))[0]


def dense_device(
    row_count,
    col_count,
    features,
    weight,
    adjacency,
    block_rows,
    block_cols,
    live_blocks,
    part_gains,
    partition,
    cotangent,
):
    share, width = features.shape
    step = share // CHUNKS
    row_blocks = share * col_count // BLOCK
    at = jnp.stack([lax.axis_index("row"), lax.axis_index("col")]).astype(jnp.int32)
    gathered = [features] + [swap(features, "row", r, row_count) for r in range(1, row_count)]
    layout = (col_count, share // BLOCK, step // BLOCK)
    tile = build_tile(
        at, adjacency, block_rows, block_cols, live_blocks, row_blocks, share * row_count // BLOCK, layout
    )
    part_count = part_gains.shape[0]
    members = (
        partition[None, :] == jnp.arange(part_count, dtype=jnp.int32)[:, None]
    ).astype(jnp.float32)
    row_gains = lax.dot_general(
        members, part_gains, (((0,), (0,)), ((), ())), precision=lax.Precision.HIGHEST
    )
    upstream = wide(cotangent) * row_gains

    order = block_order(col_count)
    col_bits = bits_of(col_count)
    chunks = range(CHUNKS)
    early = row_count // 2
    sums = [forward(n, tile, gathered[:early], 0) for n in chunks]
    pending = []
    for n in chunks:
        send, rest = forward(n, tile, gathered[early:], early, sums[n])
        other = swap(send, "col", col_bits[0], col_count)
        kept = enumerate(order[len(order) // 2 :])
        pending.append({k: [(rest, t * step), (other, t * step)] for t, k in kept})
    last = None
    for bit in col_bits[1:]:
        for terms in pending:
            blocks = sorted((k for k in terms if k & bit), reverse=True)
            sums = [terms.pop(k) for k in blocks]
            if last is not None:
                x, start = sums[0][-1]
                sums[0][-1] = (after(x, last), start)
            outs = combine(step, sums)
            last = outs[0]
            for k, out in zip(blocks, outs):
                terms[k ^ bit].append((swap(out, "col", bit, col_count), 0))
    gated, held = [], []
    for n in chunks:
        gated.append(gate(n, after(upstream, last), weight, pending[n][0]))
        last = gated[-1][0]
        held.append({0: last})
    scale = 1.0 / math.sqrt(share * row_count * col_count)
    local = [(rows, grad, summed) for _, grad, rows, summed in gated]
    message, out = local_terms(at, members, cotangent, local)
    other = swap(out, "col", col_bits[0], col_count)
    messages = [add_messages(part_count, message, other)]
    for bit in reversed(col_bits[1:]):
        for n in chunks:
            for k in list(held[n]):
                sent = held[n][k]
                if k and n == 0:
                    sent = after(sent, message)
                if k and n:
                    sent = after(sent, messages[0], *held[n].values())
                held[n][k ^ bit] = swap(sent, "col", bit, col_count)
    stages = [("row", bit, row_count) for bit in bits_of(row_count)]
    stages += [("col", bit, col_count) for bit in col_bits[1:]]
    for stage in stages:
        messages.append(add_messages(part_count, messages[-1], swap(messages[-1], *stage)))
    other = swap(messages[-1], "col", col_bits[0], col_count)
    weight_grad, gain_grad = totals(part_count, scale, at, messages[-1], other)

    layer_out = output(after(row_gains, messages[4]), [g[3] for g in gated])
    sums = []
    bit = col_bits[0]
    for n in chunks:
        blocks, places = [], []
        *ready, late = held[n]
        for group in (ready, [late]):
            sent = jnp.concatenate([held[n][k] for k in group], axis=0)
            if n and group is not ready:
                sent = after(sent, messages[1])
            arrived = swap(sent, "col", bit, col_count)
            for t, k in enumerate(group):
                blocks += [held[n][k], arrived]
                places += [(0, order.index(k) * step, step), (t * step, order.index(k ^ bit) * step, step)]
        rows = list(range(row_count))
        if n < CHUNKS - 1:
            kinds = [jnp.float32] * row_count
            *sums, _ = backward(n, rows, kinds, tile, blocks, places, sums, share)
    parts = [None] * row_count
    farthest = row_count - 1
    for targets in ([farthest], rows[1:farthest], [0]):
        if not targets:
            continue
        kinds = [jnp.float32 if r == 0 else jnp.bfloat16 for r in targets]
        *outs, panel = backward(
            CHUNKS - 1, targets, kinds, tile, blocks, places, [sums[r] for r in targets], share
        )
        blocks, places = [after(panel, messages[3], *outs)], [(0, 0, panel.shape[0])]
        for r, out in zip(targets, outs):
            parts[r] = swap(out, "row", r, row_count) if r else out
    feature_grad = finish(parts)

    return (layer_out, feature_grad, weight_grad, gain_grad)


def slot_sum(tile_values, row_index, col_index, live_count, panels, out_blocks, forward_way):
    slot_count = tile_values.shape[0]
    feature_width = panels.shape[1]
    panel_blocks = panels.reshape(-1, BLOCK, feature_width)

    def one_slot(slot, totals):
        values = lax.dynamic_index_in_dim(tile_values, slot, 0, keepdims=False)
        source, target = col_index[slot], row_index[slot]
        if not forward_way:
            values, source, target = values.T, target, source
        panel = lax.dynamic_index_in_dim(panel_blocks, source, 0, keepdims=False)
        product = jnp.dot(values, panel, preferred_element_type=jnp.float32)
        return totals.at[target].add(product)

    start = jnp.zeros((out_blocks, BLOCK, feature_width), jnp.float32)
    totals = lax.fori_loop(0, jnp.minimum(live_count, slot_count), one_slot, start)
    return totals.reshape(out_blocks * BLOCK, feature_width)


def slot_device(
    features,
    weight,
    adjacency,
    block_rows,
    block_cols,
    live_blocks,
    part_gains,
    partition,
    cotangent,
):
    node_count = features.shape[0]
    row_total = node_count * lax.axis_size("col") // BLOCK
    col_total = node_count * lax.axis_size("row") // BLOCK
    slots = (adjacency[0, 0], block_rows[0, 0], block_cols[0, 0], live_blocks[0, 0])
    hidden = jnp.dot(features, weight, preferred_element_type=jnp.float32).astype(jnp.bfloat16)
    panels = lax.all_gather(hidden, "row", axis=0, tiled=True)
    member = (
        partition[:, None] == jnp.arange(part_gains.shape[0], dtype=jnp.int32)[None, :]
    ).astype(jnp.float32)
    row_gains = jnp.dot(member, part_gains, precision=lax.Precision.HIGHEST)
    upstream = cotangent.astype(jnp.float32) * row_gains
    partial_rows = slot_sum(*slots, panels, row_total, True)
    summed = lax.psum_scatter(
        partial_rows.astype(jnp.bfloat16), "col", scatter_dimension=0, tiled=True
    ).astype(jnp.float32)
    local_grad = (upstream * silu_slope(summed)).astype(jnp.bfloat16)
    agg_grad = lax.all_gather(local_grad, "col", axis=0, tiled=True)
    activated = jax.nn.silu(summed)
    layer_out = (activated * row_gains).astype(jnp.bfloat16)
    partial_cols = slot_sum(*slots, agg_grad, col_total, False)
    hidden_grad = lax.psum_scatter(
        partial_cols.astype(jnp.bfloat16), "row", scatter_dimension=0, tiled=True
    )
    feature_grad = lax.dot_general(
        hidden_grad, weight, (((1,), (1,)), ((), ())), preferred_element_type=jnp.float32
    ).astype(jnp.bfloat16)
    weight_part = lax.dot_general(
        features, hidden_grad, (((0,), (0,)), ((), ())), preferred_element_type=jnp.float32
    )
    part_terms = jnp.dot(
        member.T, cotangent.astype(jnp.float32) * activated, precision=lax.Precision.HIGHEST
    )
    part_sizes = jnp.sum(member, axis=0)
    weight_total, part_total, size_total = lax.psum(
        (weight_part, part_terms, part_sizes), ("row", "col")
    )
    total_nodes = node_count * lax.axis_size("row") * lax.axis_size("col")
    weight_grad = weight_total / jnp.sqrt(jnp.float32(total_nodes))
    gain_grad = part_total / jnp.sqrt(size_total)[:, None]
    return (layer_out, feature_grad, weight_grad, gain_grad)


def solution(mesh):
    row_count, col_count = mesh.shape["row"], mesh.shape["col"]

    def per_device(features, *others):
        share = features.shape[0]
        tile_bytes = 2 * share**2 * row_count * col_count
        sizes = (row_count // 2, col_count // 2, share // (BLOCK * CHUNKS))
        whole = share % (BLOCK * CHUNKS) == 0 and others[1].shape[2] % GROUP == 0
        if tile_bytes <= 20 * MIB and whole and all(n & (n - 1) == 0 < n for n in sizes):
            return dense_device(row_count, col_count, features, *others)
        return slot_device(features, *others)

    in_specs = (
        P(("row", "col"), None),
        P(),
        P("row", "col", None, None, None),
        P("row", "col", None),
        P("row", "col", None),
        P("row", "col"),
        P(),
        P(("row", "col")),
        P(("row", "col"), None),
    )
    out_specs = (P(("row", "col"), None), P(("row", "col"), None), P(), P())
    return jax.shard_map(
        per_device, mesh=mesh, in_specs=in_specs, out_specs=out_specs, check_vma=False
    )
```

```python
import functools
import math

import jax
import jax.numpy as jnp
from jax import lax
from jax.experimental import pallas as pl
from jax.experimental.pallas import tpu as pltpu
from jax.sharding import PartitionSpec as P

BLOCK = 128
GROUP = 16
HEAVY = 16
CHUNKS = 2
MIB = 1 << 20
LIGHT = pl.CostEstimate(flops=1, bytes_accessed=1, transcendentals=0)


def bits_of(count):
    return [1 << b for b in range(count.bit_length() - 1)]


def shift_of(count):
    return count.bit_length() - 1


def block_order(count):
    return list(range(1, count, 2)) + list(range(0, count, 2))


def build_kernel(layout, at_ref, live_ref, rows_ref, cols_ref, slots_ref, tile_ref, buf, total, counts, most, sems):
    owners, per_owner, per_chunk = layout
    live = live_ref[0, 0]
    groups = (live + GROUP - 1) // GROUP
    row_blocks, col_blocks = tile_ref.shape[0] // BLOCK, tile_ref.shape[1] // BLOCK

    def fetch(group):
        return pltpu.make_async_copy(
            slots_ref.at[0, 0, pl.ds(group * GROUP, GROUP)], buf.at[group], sems.at[group]
        )

    @pl.loop(0, groups)
    def _(group):
        fetch(group).start()

    zeros = jnp.zeros((BLOCK, tile_ref.shape[1]), tile_ref.dtype)
    most[0] = 0

    @pl.loop(0, row_blocks)
    def _(r):
        tile_ref[pl.ds(pl.multiple_of(r * BLOCK, BLOCK), BLOCK), :] = zeros
        for c in range(col_blocks):
            counts[r * col_blocks + c] = 0

    own_row, own_col = at_ref[0], at_ref[1]

    def place(index):
        row = rows_ref[0, 0, index]
        k, inner = (row >> shift_of(per_owner)) ^ own_col, row & (per_owner - 1)
        k = ((k & 1) ^ 1) * (owners // 2) + (k >> 1)
        chunk, inner = inner >> shift_of(per_chunk), inner & (per_chunk - 1)
        row = (((chunk << shift_of(owners)) + k) << shift_of(per_chunk)) + inner
        return row, cols_ref[0, 0, index] ^ (own_row << shift_of(per_owner))

    def block(row, col):
        top, left = pl.multiple_of(row * BLOCK, BLOCK), pl.multiple_of(col * BLOCK, BLOCK)
        return pl.ds(top, BLOCK), pl.ds(left, BLOCK)

    @pl.loop(0, groups)
    def _(group):
        fetch(group).wait()

        def add(s):
            row, col = place(group * GROUP + s)
            here = counts[row * col_blocks + col] + 1
            counts[row * col_blocks + col] = here
            tile_ref[block(row, col)] += buf[group, s]
            return here

        here = live - group * GROUP

        @pl.when(here >= GROUP)
        def _():
            most[0] = functools.reduce(jnp.maximum, [add(s) for s in range(GROUP)], most[0])

        @pl.when(here < GROUP)
        def _():
            @pl.loop(0, here)
            def _(s):
                most[0] = jnp.maximum(most[0], add(s))

    @pl.when(most[0] > HEAVY)
    def _():
        @pl.loop(0, live)
        def _(index):
            p_row, p_col = place(index)
            p = p_row * col_blocks + p_col

            @pl.when(counts[p] > HEAVY)
            def _():
                counts[p] = 0
                total[...] = jnp.zeros_like(total)

                @pl.loop(index, live)
                def _(other):
                    row, col = place(other)

                    @pl.when(row * col_blocks + col == p)
                    def _():
                        total[...] += buf[other >> shift_of(GROUP), other & (GROUP - 1)].astype(jnp.float32)

                tile_ref[block(p_row, p_col)] = total[...].astype(tile_ref.dtype)


def build_tile(at, slots, rows, cols, live, row_blocks, col_blocks, layout):
    smem = pl.BlockSpec(memory_space=pltpu.SMEM)
    vmem = pl.BlockSpec(memory_space=pltpu.VMEM)
    groups = slots.shape[2] // GROUP
    return pl.pallas_call(
        functools.partial(build_kernel, layout),
        out_shape=pltpu.VMEM((row_blocks * BLOCK, col_blocks * BLOCK), jnp.bfloat16),
        in_specs=[smem, smem, smem, smem, pl.BlockSpec(memory_space=pl.ANY)],
        out_specs=vmem,
        scratch_shapes=[
            pltpu.VMEM((groups, GROUP, BLOCK, BLOCK), jnp.bfloat16),
            pltpu.VMEM((BLOCK, BLOCK), jnp.float32),
            pltpu.SMEM((row_blocks * col_blocks,), jnp.int32),
            pltpu.SMEM((1,), jnp.int32),
            pltpu.SemaphoreType.DMA((groups,)),
        ],
        compiler_params=pltpu.CompilerParams(vmem_limit_bytes=36 * MIB),
        cost_estimate=pl.CostEstimate(flops=0, bytes_accessed=20 * MIB, transcendentals=0),
        name="build_tile",
    )(at, live, rows, cols, slots)


def forward_kernel(chunk, first, tile_ref, *refs):
    *feature_refs, panel = refs
    if first:
        before_ref, (*feature_refs, send_ref, rest_ref) = feature_refs[0], feature_refs[1:]
    else:
        *feature_refs, sum_ref = feature_refs
    share = feature_refs[0].shape[0]
    for r, feature_ref in enumerate(feature_refs):
        panel[r * share : (r + 1) * share, :] = feature_ref[...]
    rows = tile_ref.shape[0] // CHUNKS
    half = rows // 2
    for m in range(0, rows, half):
        block = tile_ref[chunk * rows + m : chunk * rows + m + half, first * share : first * share + panel.shape[0]]
        product = jnp.dot(block, panel[...], preferred_element_type=jnp.float32)
        if first:
            into = rest_ref if m else send_ref
            into[...] = (before_ref[m : m + half, :] + product).astype(jnp.bfloat16)
        else:
            sum_ref[m : m + half, :] = product


def forward(chunk, tile, features, first, before=None):
    share, width = features[0].shape
    rows = tile.shape[0] // CHUNKS
    vmem = pl.BlockSpec(memory_space=pltpu.VMEM)
    if first:
        given, out_shape = [before, *features], [pltpu.VMEM((rows // 2, width), jnp.bfloat16)] * 2
    else:
        given, out_shape = features, pltpu.VMEM((rows, width), jnp.float32)
    return pl.pallas_call(
        functools.partial(forward_kernel, chunk, first),
        out_shape=out_shape,
        in_specs=[vmem] * (1 + len(given)),
        out_specs=[vmem] * 2 if first else vmem,
        scratch_shapes=[pltpu.VMEM((len(features) * share, width), jnp.bfloat16)],
        compiler_params=pltpu.CompilerParams(vmem_limit_bytes=8 * MIB),
        cost_estimate=pl.CostEstimate(
            flops=2 * rows * len(features) * share * width, bytes_accessed=0, transcendentals=0
        ),
        name="forward",
    )(tile, *given)


def silu_slope(values):
    sig = jax.nn.sigmoid(values)
    return sig * (1.0 + values * (1.0 - sig))


def wide(values):
    return values.astype(jnp.float32)


def dot_last(left, right):
    return lax.dot_general(left, right, (((1,), (1,)), ((), ())), preferred_element_type=jnp.float32)


def combine_kernel(specs, *refs):
    out_refs = refs[-len(specs) :]
    for spec, out_ref in zip(specs, out_refs):
        total = None
        for source, start in spec:
            term = wide(refs[source][start : start + out_ref.shape[0], :])
            total = term if total is None else total + term
        out_ref[...] = total.astype(out_ref.dtype)


def combine(step, sums):
    sources = list({id(x): x for terms in sums for x, _ in terms}.values())
    at = {id(x): i for i, x in enumerate(sources)}
    specs = [[(at[id(x)], start) for x, start in terms] for terms in sums]
    vmem = pl.BlockSpec(memory_space=pltpu.VMEM)
    return pl.pallas_call(
        functools.partial(combine_kernel, specs),
        out_shape=[pltpu.VMEM((step, sources[0].shape[1]), jnp.bfloat16)] * len(sums),
        in_specs=[vmem] * len(sources),
        out_specs=[vmem] * len(sums),
        compiler_params=pltpu.CompilerParams(vmem_limit_bytes=4 * MIB),
        cost_estimate=LIGHT,
        name="combine",
    )(*sources)


def gate_kernel(chunk, starts, upstream_ref, weight_ref, *refs):
    *term_refs, turned_ref, grad_ref, rows_ref, summed_ref = refs
    step = grad_ref.shape[0]
    rows = None
    for term_ref, start in zip(term_refs, starts):
        term = wide(term_ref[start : start + step, :])
        rows = term if rows is None else rows + term
    high = rows.astype(jnp.bfloat16)
    low = (rows - wide(high)).astype(jnp.bfloat16)
    weight = weight_ref[...]
    summed = jnp.dot(high, weight, preferred_element_type=jnp.float32) + jnp.dot(
        low, weight, preferred_element_type=jnp.float32
    )
    upstream = upstream_ref[chunk * step : (chunk + 1) * step, :]
    grad = (upstream * silu_slope(summed)).astype(jnp.bfloat16)
    turned_ref[...] = dot_last(grad, weight).astype(jnp.bfloat16)
    grad_ref[...] = grad
    rows_ref[...] = high
    summed_ref[...] = summed


def gate(chunk, upstream, weight, terms):
    shape = (upstream.shape[0] // CHUNKS, upstream.shape[1])
    vmem = pl.BlockSpec(memory_space=pltpu.VMEM)
    return pl.pallas_call(
        functools.partial(gate_kernel, chunk, [start for _, start in terms]),
        out_shape=[pltpu.VMEM(shape, jnp.bfloat16)] * 3 + [pltpu.VMEM(shape, jnp.float32)],
        in_specs=[vmem] * (2 + len(terms)),
        out_specs=[vmem] * 4,
        compiler_params=pltpu.CompilerParams(vmem_limit_bytes=8 * MIB),
        cost_estimate=LIGHT,
        name="gate",
    )(upstream, weight, *(x for x, _ in terms))


def pack(values, exact_rows):
    exact = values[values.shape[0] - exact_rows :]
    high = exact.astype(jnp.bfloat16)
    low = (exact - wide(high)).astype(jnp.bfloat16)
    return jnp.concatenate([values[: -exact_rows].astype(jnp.bfloat16), high, low], axis=0)


def unpack(message, exact_rows):
    values = wide(message)
    rows = message.shape[0] - 2 * exact_rows
    exact = values[rows : rows + exact_rows] + values[rows + exact_rows :]
    return jnp.concatenate([values[:rows], exact], axis=0)


def local_sums(chunk, members_ref, cotangent_ref, rows_ref, grad_ref, summed_ref):
    step = rows_ref.shape[0]
    at = slice(chunk * step, (chunk + 1) * step)
    summed = summed_ref[...]
    activated = summed * jax.nn.sigmoid(summed)
    weight_part = lax.dot_general(
        rows_ref[...], grad_ref[...], (((0,), (0,)), ((), ())), preferred_element_type=jnp.float32
    )
    members = members_ref[:, at]
    part_terms = jnp.dot(
        members,
        wide(cotangent_ref[at, :]) * activated,
        precision=lax.Precision.HIGHEST,
        preferred_element_type=jnp.float32,
    )
    sizes = jnp.sum(members, axis=1, keepdims=True)
    return jnp.concatenate([weight_part, part_terms, jnp.broadcast_to(sizes, part_terms.shape)], axis=0)


def local_first_kernel(members_ref, cotangent_ref, *refs):
    *given, sums_ref = refs
    sums_ref[...] = local_sums(0, members_ref, cotangent_ref, *given)


def local_last_kernel(at_ref, members_ref, cotangent_ref, before_ref, *refs):
    *given, keep_ref, send_ref, sums = refs
    terms = local_sums(CHUNKS - 1, members_ref, cotangent_ref, *given)
    sums[...] = before_ref[...] + terms
    core = at_ref[1] & 1
    count = members_ref.shape[0]
    width = sums.shape[1]
    rows = width // 2
    for half, message_ref in ((core, keep_ref), (1 - core, send_ref)):
        top = sums[pl.ds(pl.multiple_of(half * rows, rows), rows), :]
        bottom = sums[pl.ds(pl.multiple_of(width + half * count, count), count), :]
        message_ref[...] = pack(jnp.concatenate([top, bottom], axis=0), count)


def local_terms(at, members, cotangent, chunks):
    width = cotangent.shape[1]
    count = members.shape[0]
    vmem = pl.BlockSpec(memory_space=pltpu.VMEM)
    smem = pl.BlockSpec(memory_space=pltpu.SMEM)
    first, last = chunks
    sums = jax.ShapeDtypeStruct((width + 2 * count, width), jnp.float32)
    before = pl.pallas_call(
        local_first_kernel,
        out_shape=pltpu.VMEM(sums.shape, sums.dtype),
        in_specs=[vmem] * 5,
        out_specs=vmem,
        compiler_params=pltpu.CompilerParams(vmem_limit_bytes=8 * MIB),
        cost_estimate=LIGHT,
        name="local_first",
    )(members, cotangent, *first)
    message = pltpu.VMEM((width // 2 + 2 * count, width), jnp.bfloat16)
    return pl.pallas_call(
        local_last_kernel,
        out_shape=[message, message],
        in_specs=[smem] + [vmem] * 6,
        out_specs=[vmem] * 2,
        scratch_shapes=[pltpu.VMEM(sums.shape, sums.dtype)],
        compiler_params=pltpu.CompilerParams(vmem_limit_bytes=8 * MIB),
        cost_estimate=LIGHT,
        name="local_last",
    )(at, members, cotangent, before, *last)


def output_kernel(gains_ref, *refs):
    *summed_refs, out_ref = refs
    step = summed_refs[0].shape[0]
    for n, summed_ref in enumerate(summed_refs):
        at = slice(n * step, (n + 1) * step)
        summed = summed_ref[...]
        out_ref[at, :] = (summed * jax.nn.sigmoid(summed) * gains_ref[at, :]).astype(out_ref.dtype)


def output(gains, summed):
    vmem = pl.BlockSpec(memory_space=pltpu.VMEM)
    return pl.pallas_call(
        output_kernel,
        out_shape=jax.ShapeDtypeStruct(gains.shape, jnp.bfloat16),
        in_specs=[vmem] * (1 + len(summed)),
        out_specs=vmem,
        compiler_params=pltpu.CompilerParams(vmem_limit_bytes=8 * MIB),
        cost_estimate=LIGHT,
        name="output",
    )(gains, *summed)


def add_kernel(exact_rows, own_ref, other_ref, out_ref):
    out_ref[...] = pack(
        unpack(own_ref[...], exact_rows) + unpack(other_ref[...], exact_rows), exact_rows
    )


def add_messages(exact_rows, own, other):
    vmem = pl.BlockSpec(memory_space=pltpu.VMEM)
    return pl.pallas_call(
        functools.partial(add_kernel, exact_rows),
        out_shape=pltpu.VMEM(own.shape, jnp.bfloat16),
        in_specs=[vmem] * 2,
        out_specs=vmem,
        compiler_params=pltpu.CompilerParams(vmem_limit_bytes=4 * MIB),
        cost_estimate=LIGHT,
        name="add_messages",
    )(own, other)


def totals_kernel(exact_rows, scale, at_ref, own_ref, other_ref, weight_ref, gain_ref, exact):
    core = at_ref[1] & 1
    rows = weight_ref.shape[0] // 2
    for half, message_ref in ((core, own_ref), (1 - core, other_ref)):
        values = unpack(message_ref[...], exact_rows)
        weight_ref[pl.ds(pl.multiple_of(half * rows, rows), rows), :] = values[:rows] * scale
        exact[pl.ds(pl.multiple_of(half * exact_rows, exact_rows), exact_rows), :] = values[rows:]
    gain_ref[...] = exact[:exact_rows, :] / jnp.sqrt(exact[exact_rows:, :])


def totals(exact_rows, scale, at, own, other):
    width = own.shape[1]
    vmem = pl.BlockSpec(memory_space=pltpu.VMEM)
    smem = pl.BlockSpec(memory_space=pltpu.SMEM)
    return pl.pallas_call(
        functools.partial(totals_kernel, exact_rows, scale),
        out_shape=[
            jax.ShapeDtypeStruct((width, width), jnp.float32),
            jax.ShapeDtypeStruct((exact_rows, width), jnp.float32),
        ],
        in_specs=[smem] + [vmem] * 2,
        out_specs=[vmem] * 2,
        scratch_shapes=[pltpu.VMEM((2 * exact_rows, width), jnp.float32)],
        compiler_params=pltpu.CompilerParams(vmem_limit_bytes=4 * MIB),
        cost_estimate=LIGHT,
        name="totals",
    )(at, own, other)


def backward_kernel(chunk, targets, places, tile_ref, *refs):
    given, out_refs = refs[: -len(targets) - 1], refs[-len(targets) - 1 :]
    before_refs, block_refs = given[: len(given) - len(places)], given[len(given) - len(places) :]
    *part_refs, panel = out_refs
    for block_ref, (source, target, rows) in zip(block_refs, places):
        panel[target : target + rows, :] = block_ref[source : source + rows, :]
    share = part_refs[0].shape[0]
    depth = panel.shape[0]
    for i, r in enumerate(targets):
        product = lax.dot_general(
            tile_ref[chunk * depth : (chunk + 1) * depth, r * share : (r + 1) * share],
            panel[...],
            (((0,), (0,)), ((), ())),
            preferred_element_type=jnp.float32,
        )
        if before_refs:
            product = product + before_refs[i][...]
        part_refs[i][...] = product.astype(part_refs[i].dtype)


def backward(chunk, targets, kinds, tile, blocks, places, before, share):
    width = blocks[0].shape[1]
    depth = tile.shape[0] // CHUNKS
    vmem = pl.BlockSpec(memory_space=pltpu.VMEM)
    scale = 2 if chunk == 0 else 8 if len(targets) > 1 else 1
    flops = scale * depth * len(targets) * share * width
    return pl.pallas_call(
        functools.partial(backward_kernel, chunk, targets, places),
        out_shape=[pltpu.VMEM((share, width), kind) for kind in kinds]
        + [pltpu.VMEM((depth, width), jnp.bfloat16)],
        in_specs=[vmem] * (1 + len(before) + len(blocks)),
        out_specs=[vmem] * (len(targets) + 1),
        compiler_params=pltpu.CompilerParams(vmem_limit_bytes=8 * MIB),
        cost_estimate=pl.CostEstimate(flops=flops, bytes_accessed=0, transcendentals=0),
        name="backward",
    )(tile, *before, *blocks)


def finish_kernel(*refs):
    *part_refs, out_ref = refs
    total = None
    for part_ref in part_refs:
        term = wide(part_ref[...])
        total = term if total is None else total + term
    out_ref[...] = total.astype(out_ref.dtype)


def finish(parts):
    vmem = pl.BlockSpec(memory_space=pltpu.VMEM)
    return pl.pallas_call(
        finish_kernel,
        out_shape=jax.ShapeDtypeStruct(parts[0].shape, jnp.bfloat16),
        in_specs=[vmem] * len(parts),
        out_specs=vmem,
        compiler_params=pltpu.CompilerParams(vmem_limit_bytes=8 * MIB),
        cost_estimate=LIGHT,
        name="finish",
    )(*parts)


def swap(values, axis, mask, count):
    return lax.ppermute(values, axis, [(d, d ^ mask) for d in range(count)])


def after(values, *others):
    return lax.optimization_barrier((values, *others))[0]


def dense_device(
    row_count,
    col_count,
    features,
    weight,
    adjacency,
    block_rows,
    block_cols,
    live_blocks,
    part_gains,
    partition,
    cotangent,
):
    share, width = features.shape
    step = share // CHUNKS
    row_blocks = share * col_count // BLOCK
    at = jnp.stack([lax.axis_index("row"), lax.axis_index("col")]).astype(jnp.int32)
    gathered = [features] + [swap(features, "row", r, row_count) for r in range(1, row_count)]
    layout = (col_count, share // BLOCK, step // BLOCK)
    tile = build_tile(
        at, adjacency, block_rows, block_cols, live_blocks, row_blocks, share * row_count // BLOCK, layout
    )
    part_count = part_gains.shape[0]
    members = (
        partition[None, :] == jnp.arange(part_count, dtype=jnp.int32)[:, None]
    ).astype(jnp.float32)
    row_gains = lax.dot_general(
        members, part_gains, (((0,), (0,)), ((), ())), precision=lax.Precision.HIGHEST
    )
    upstream = wide(cotangent) * row_gains

    order = block_order(col_count)
    col_bits = bits_of(col_count)
    chunks = range(CHUNKS)
    early = row_count // 2
    sums = [forward(n, tile, gathered[:early], 0) for n in chunks]
    pending = []
    for n in chunks:
        send, rest = forward(n, tile, gathered[early:], early, sums[n])
        other = swap(send, "col", col_bits[0], col_count)
        kept = enumerate(order[len(order) // 2 :])
        pending.append({k: [(rest, t * step), (other, t * step)] for t, k in kept})
    last = None
    for bit in col_bits[1:]:
        for terms in pending:
            blocks = sorted((k for k in terms if k & bit), reverse=True)
            sums = [terms.pop(k) for k in blocks]
            if last is not None:
                x, start = sums[0][-1]
                sums[0][-1] = (after(x, last), start)
            outs = combine(step, sums)
            last = outs[0]
            for k, out in zip(blocks, outs):
                terms[k ^ bit].append((swap(out, "col", bit, col_count), 0))
    gated, held = [], []
    for n in chunks:
        gated.append(gate(n, after(upstream, last), weight, pending[n][0]))
        last = gated[-1][0]
        held.append({0: last})
    scale = 1.0 / math.sqrt(share * row_count * col_count)
    local = [(rows, grad, summed) for _, grad, rows, summed in gated]
    message, out = local_terms(at, members, cotangent, local)
    other = swap(out, "col", col_bits[0], col_count)
    messages = [add_messages(part_count, message, other)]
    for bit in reversed(col_bits[1:]):
        for n in chunks:
            for k in list(held[n]):
                sent = held[n][k]
                if k and n == 0:
                    sent = after(sent, message)
                if k and n:
                    sent = after(sent, messages[0], *held[n].values())
                held[n][k ^ bit] = swap(sent, "col", bit, col_count)
    stages = [("row", bit, row_count) for bit in bits_of(row_count)]
    stages += [("col", bit, col_count) for bit in col_bits[1:]]
    for stage in stages[:-1]:
        messages.append(add_messages(part_count, messages[-1], swap(messages[-1], *stage)))
    sums = []
    bit = col_bits[0]
    for n in chunks:
        blocks, places = [], []
        *ready, late = held[n]
        for group in (ready, [late]):
            sent = jnp.concatenate([held[n][k] for k in group], axis=0)
            if n and group is not ready:
                sent = after(sent, messages[1])
            arrived = swap(sent, "col", bit, col_count)
            for t, k in enumerate(group):
                blocks += [held[n][k], arrived]
                places += [(0, order.index(k) * step, step), (t * step, order.index(k ^ bit) * step, step)]
        rows = list(range(row_count))
        if n < CHUNKS - 1:
            kinds = [jnp.float32] * row_count
            *sums, _ = backward(n, rows, kinds, tile, blocks, places, sums, share)
    parts = [None] * row_count
    farthest = row_count - 1
    for targets in ([farthest], rows[1:farthest], [0]):
        if not targets:
            continue
        kinds = [jnp.float32 if r == 0 else jnp.bfloat16 for r in targets]
        *outs, panel = backward(
            CHUNKS - 1, targets, kinds, tile, blocks, places, [sums[r] for r in targets], share
        )
        blocks, places = [after(panel, messages[3], *outs)], [(0, 0, panel.shape[0])]
        for r, out in zip(targets, outs):
            parts[r] = swap(out, "row", r, row_count) if r else out
    arrived = swap(messages[-1], *stages[-1])
    own = after(messages[-1], parts[0])
    messages.append(add_messages(part_count, own, arrived))
    other = swap(messages[-1], "col", col_bits[0], col_count)
    weight_grad, gain_grad = totals(part_count, scale, at, messages[-1], other)
    feature_grad = finish(parts)
    layer_out = output(after(row_gains, messages[-1]), [g[3] for g in gated])

    return (layer_out, feature_grad, weight_grad, gain_grad)


def slot_sum(tile_values, row_index, col_index, live_count, panels, out_blocks, forward_way):
    slot_count = tile_values.shape[0]
    feature_width = panels.shape[1]
    panel_blocks = panels.reshape(-1, BLOCK, feature_width)

    def one_slot(slot, totals):
        values = lax.dynamic_index_in_dim(tile_values, slot, 0, keepdims=False)
        source, target = col_index[slot], row_index[slot]
        if not forward_way:
            values, source, target = values.T, target, source
        panel = lax.dynamic_index_in_dim(panel_blocks, source, 0, keepdims=False)
        product = jnp.dot(values, panel, preferred_element_type=jnp.float32)
        return totals.at[target].add(product)

    start = jnp.zeros((out_blocks, BLOCK, feature_width), jnp.float32)
    totals = lax.fori_loop(0, jnp.minimum(live_count, slot_count), one_slot, start)
    return totals.reshape(out_blocks * BLOCK, feature_width)


def slot_device(
    features,
    weight,
    adjacency,
    block_rows,
    block_cols,
    live_blocks,
    part_gains,
    partition,
    cotangent,
):
    node_count = features.shape[0]
    row_total = node_count * lax.axis_size("col") // BLOCK
    col_total = node_count * lax.axis_size("row") // BLOCK
    slots = (adjacency[0, 0], block_rows[0, 0], block_cols[0, 0], live_blocks[0, 0])
    hidden = jnp.dot(features, weight, preferred_element_type=jnp.float32).astype(jnp.bfloat16)
    panels = lax.all_gather(hidden, "row", axis=0, tiled=True)
    member = (
        partition[:, None] == jnp.arange(part_gains.shape[0], dtype=jnp.int32)[None, :]
    ).astype(jnp.float32)
    row_gains = jnp.dot(member, part_gains, precision=lax.Precision.HIGHEST)
    upstream = cotangent.astype(jnp.float32) * row_gains
    partial_rows = slot_sum(*slots, panels, row_total, True)
    summed = lax.psum_scatter(
        partial_rows.astype(jnp.bfloat16), "col", scatter_dimension=0, tiled=True
    ).astype(jnp.float32)
    local_grad = (upstream * silu_slope(summed)).astype(jnp.bfloat16)
    agg_grad = lax.all_gather(local_grad, "col", axis=0, tiled=True)
    activated = jax.nn.silu(summed)
    layer_out = (activated * row_gains).astype(jnp.bfloat16)
    partial_cols = slot_sum(*slots, agg_grad, col_total, False)
    hidden_grad = lax.psum_scatter(
        partial_cols.astype(jnp.bfloat16), "row", scatter_dimension=0, tiled=True
    )
    feature_grad = lax.dot_general(
        hidden_grad, weight, (((1,), (1,)), ((), ())), preferred_element_type=jnp.float32
    ).astype(jnp.bfloat16)
    weight_part = lax.dot_general(
        features, hidden_grad, (((0,), (0,)), ((), ())), preferred_element_type=jnp.float32
    )
    part_terms = jnp.dot(
        member.T, cotangent.astype(jnp.float32) * activated, precision=lax.Precision.HIGHEST
    )
    part_sizes = jnp.sum(member, axis=0)
    weight_total, part_total, size_total = lax.psum(
        (weight_part, part_terms, part_sizes), ("row", "col")
    )
    total_nodes = node_count * lax.axis_size("row") * lax.axis_size("col")
    weight_grad = weight_total / jnp.sqrt(jnp.float32(total_nodes))
    gain_grad = part_total / jnp.sqrt(size_total)[:, None]
    return (layer_out, feature_grad, weight_grad, gain_grad)


def solution(mesh):
    row_count, col_count = mesh.shape["row"], mesh.shape["col"]

    def per_device(features, *others):
        share = features.shape[0]
        tile_bytes = 2 * share**2 * row_count * col_count
        sizes = (row_count // 2, col_count // 2, share // (BLOCK * CHUNKS))
        whole = share % (BLOCK * CHUNKS) == 0 and others[1].shape[2] % GROUP == 0
        if tile_bytes <= 20 * MIB and whole and all(n & (n - 1) == 0 < n for n in sizes):
            return dense_device(row_count, col_count, features, *others)
        return slot_device(features, *others)

    in_specs = (
        P(("row", "col"), None),
        P(),
        P("row", "col", None, None, None),
        P("row", "col", None),
        P("row", "col", None),
        P("row", "col"),
        P(),
        P(("row", "col")),
        P(("row", "col"), None),
    )
    out_specs = (P(("row", "col"), None), P(("row", "col"), None), P(), P())
    return jax.shard_map(
        per_device, mesh=mesh, in_specs=in_specs, out_specs=out_specs, check_vma=False
    )
```
